32 devices in a mesh: tile: 8 (over z, y), spec: 4 (over x, core).
Axes of the slice: x: 2, y: 2, z: 4, core: 2. Of those that a mesh axis runs over, the one named last changes fastest.
Arguments:
- latent: bfloat16 [32, 2048, 1024], P(None, ('tile', 'spec')), may hold values from -6 to 6
- basis: bfloat16 [224, 32], replicated, may hold values from -1 to 1
- response: bfloat16 [8, 224], replicated, may hold values from -0.375 to 0.375
- hyper_obs: bfloat16 [224, 512, 256], P('spec', 'tile'), may hold values from -6 to 6
- multi_obs: bfloat16 [8, 2048, 1024], P(None, ('tile', 'spec')), may hold values from -6 to 6
Outputs:
- z_next: bfloat16 [32, 2048, 1024], P(None, ('tile', 'spec'))
- hs_residual: bfloat16 [224, 512, 256], P('spec', 'tile')
The draws below stay inside these ranges and needn't reach their ends.
All inputs are finite; a program needn't handle non-finite values.
Results may differ from the reference program's by a relative error of at most 0.0054.
Values may be sent and summed in bfloat16 or wider, within the bound.
A program may use at most 128 MiB of HBM per device.

```python
import jax
import jax.numpy as jnp
from jax import lax

BANDS = 224
SUBSPACE = 32
MS_BANDS = 8
DECIM = 4
HALO = 128
ROWS_DEV = 256
COLS = 1024
ROWS = 2048
LOW_ROWS = 512
LOW_COLS = 256
N_TILE = 8
N_SPEC = 4


def steps_of(own_key, dims, cuts, smallest, largest):
    factor_of = 1.0
    for position, parts in cuts:
        heights = jax.random.uniform(jax.random.fold_in(jax.random.fold_in(own_key, 6), position), (parts,), jnp.float32, smallest / len(cuts), largest / len(cuts))
        factor_of = factor_of * jnp.repeat(jnp.exp(heights), dims[position] // parts).reshape((-1,) + (1,) * (len(dims) - 1 - position))
    return factor_of


def bell_draw(stream_key, extent, scale, reach, shards=(), held_as=jnp.bfloat16):
    gain = steps_of(stream_key, extent, shards, -0.22, 0.18) if shards else 1.0
    result = jax.random.normal(stream_key, extent, jnp.float32) * scale * gain
    return jnp.minimum(jnp.maximum(result, -reach), reach).astype(held_as)


def setup_inputs(seed: int = 0) -> dict:
    keys = jax.random.split(jax.random.key(seed), 6)
    latent = bell_draw(keys[0], (SUBSPACE, ROWS, COLS), 1.0, 6.0, ((1, 32),))
    basis = bell_draw(keys[1], (BANDS, SUBSPACE), SUBSPACE ** -0.5, 1.0)
    response = bell_draw(keys[2], (MS_BANDS, BANDS), BANDS ** -0.5, 0.375)
    hyper_obs = bell_draw(keys[3], (BANDS, LOW_ROWS, LOW_COLS), 1.0, 6.0, ((0, 4), (1, 8)))
    multi_obs = bell_draw(keys[4], (MS_BANDS, ROWS, COLS), 1.0, 6.0, ((1, 32),))
    return dict(latent=latent, basis=basis, response=response, hyper_obs=hyper_obs, multi_obs=multi_obs)


step_size = 0.3

def profile(where_at):
    narrow = DECIM / 2.0
    decay_len = 3.0 * HALO / 8.0
    ripple = jnp.cos(where_at * (jnp.pi / 7.0))
    return jnp.exp(-where_at * where_at / (2.0 * narrow * narrow)) + 0.5 * jnp.exp(-jnp.abs(where_at) / decay_len) * ripple * ripple

def kernel_values(offsets):
    every_offset = jnp.arange(-HALO, HALO + 1).astype(jnp.float32)
    energy = jnp.sqrt(jnp.sum(profile(every_offset) ** 2))
    inside = jnp.abs(offsets) <= HALO
    return jnp.where(inside, profile(offsets.astype(jnp.float32)) / energy, 0.0).astype(jnp.bfloat16)

def column_matrix(fine_count, coarse_count):
    fine_cols = jnp.arange(fine_count).astype(jnp.int32)[:, None]
    coarse = jnp.arange(coarse_count).astype(jnp.int32)[None, :]
    return kernel_values(fine_cols - DECIM * coarse)

def row_matrix(rows_local):
    coarse = jnp.arange(rows_local // DECIM).astype(jnp.int32)[:, None]
    padded = jnp.arange(rows_local + 2 * HALO).astype(jnp.int32)[None, :]
    return kernel_values(padded - HALO - DECIM * coarse)

def back_matrix(rows_local):
    fine_rows = jnp.arange(rows_local).astype(jnp.int32)[:, None]
    coarse = jnp.arange(rows_local // DECIM + 2 * (HALO // DECIM)).astype(jnp.int32)[None, :]
    return kernel_values(fine_rows - DECIM * coarse + HALO)

def reference(latent, basis, response, hyper_obs, multi_obs):
    highest = lax.Precision.HIGHEST
    column_kernel = column_matrix(COLS, COLS // DECIM).astype(jnp.float32)
    row_kernel = row_matrix(ROWS_DEV).astype(jnp.float32)
    back_kernel = back_matrix(ROWS_DEV).astype(jnp.float32)
    latent_full = latent.astype(jnp.float32)
    basis_full = basis.astype(jnp.float32)
    response_full = response.astype(jnp.float32)
    group = BANDS // N_SPEC
    coarse_rows = ROWS_DEV // DECIM
    rim_rows = HALO // DECIM
    tiles_all = jnp.arange(N_TILE).astype(jnp.int32)
    groups_all = jnp.arange(N_SPEC).astype(jnp.int32)

    def spectra_of(group_index):
        rows_basis = lax.dynamic_slice_in_dim(basis_full, group_index * group, group, 0)
        field = jnp.einsum('bk,krc->brc', rows_basis, latent_full, precision=highest)
        return lax.optimization_barrier(field.astype(jnp.bfloat16)).astype(jnp.float32)

    def multi_step(running, group_index):
        field = spectra_of(group_index)
        cols_response = lax.dynamic_slice_in_dim(response_full, group_index * group, group, 1)
        return (running + jnp.einsum('mb,brc->mrc', cols_response, field, precision=highest), None)
    running, unused = lax.scan(multi_step, jnp.zeros((MS_BANDS, ROWS, COLS), jnp.float32), groups_all)
    multi_resid = (running - multi_obs.astype(jnp.float32)).astype(jnp.bfloat16)
    multi_wide = lax.optimization_barrier(multi_resid).astype(jnp.float32)

    def blur_down(band_field):
        narrowed = jnp.dot(band_field, column_kernel, precision=highest)
        padded = jnp.pad(narrowed, ((HALO, HALO), (0, 0)))

        def one_tile(tile_index):
            window_rows = lax.dynamic_slice_in_dim(padded, tile_index * ROWS_DEV, ROWS_DEV + 2 * HALO, 0)
            return jnp.dot(row_kernel, window_rows, precision=highest)
        return lax.map(one_tile, tiles_all).reshape(LOW_ROWS, LOW_COLS)

    def spread_up(coarse_field):
        padded = jnp.pad(coarse_field, ((rim_rows, rim_rows), (0, 0)))

        def one_tile(tile_index):
            window_rows = lax.dynamic_slice_in_dim(padded, tile_index * coarse_rows, coarse_rows + 2 * rim_rows, 0)
            return jnp.dot(back_kernel, window_rows, precision=highest)
        rows_back = lax.map(one_tile, tiles_all).reshape(ROWS, LOW_COLS)
        return jnp.dot(rows_back, column_kernel.T, precision=highest)

    def main_step(gradient, group_index):
        field = spectra_of(group_index)
        observed = lax.dynamic_slice_in_dim(hyper_obs, group_index * group, group, 0).astype(jnp.float32)
        hyper_resid = (jax.vmap(blur_down)(field) - observed).astype(jnp.bfloat16)
        resid_wide = lax.optimization_barrier(hyper_resid).astype(jnp.float32)
        spread = jax.vmap(spread_up)(resid_wide)
        spread = lax.optimization_barrier(spread.astype(jnp.bfloat16)).astype(jnp.float32)
        cols_response = lax.dynamic_slice_in_dim(response_full, group_index * group, group, 1)
        multi_back = jnp.einsum('mb,mrc->brc', cols_response, multi_wide, precision=highest)
        spectral = lax.optimization_barrier((spread + multi_back).astype(jnp.bfloat16)).astype(jnp.float32)
        rows_basis = lax.dynamic_slice_in_dim(basis_full, group_index * group, group, 0)
        gradient = gradient + jnp.einsum('bk,brc->krc', rows_basis, spectral, precision=highest)
        return (gradient, hyper_resid)
    gradient, residuals = lax.scan(main_step, jnp.zeros((SUBSPACE, ROWS, COLS), jnp.float32), groups_all)
    z_next = (latent_full - step_size * gradient).astype(jnp.bfloat16)
    return (z_next, residuals.reshape(BANDS, LOW_ROWS, LOW_COLS))
```

```python
import jax
import jax.numpy as jnp
import numpy as np
from jax import lax
from jax.sharding import PartitionSpec as P

DECIM = 4
HALO = 128
RIM = HALO // DECIM
STEP = 0.3


def profile(where_at):
    narrow = np.float32(DECIM / 2.0)
    decay_len = np.float32(3.0 * HALO / 8.0)
    ripple = np.cos(where_at * np.float32(np.pi / 7.0))
    return np.exp(-where_at * where_at / (np.float32(2.0) * narrow * narrow)) + np.float32(
        0.5
    ) * np.exp(-np.abs(where_at) / decay_len) * ripple * ripple


def kernel_values(offsets):
    every_offset = np.arange(-HALO, HALO + 1).astype(np.float32)
    energy = np.sqrt(np.sum(profile(every_offset) ** 2))
    inside = np.abs(offsets) <= HALO
    return np.where(inside, profile(offsets.astype(np.float32)) / energy, np.float32(0.0)).astype(
        jnp.bfloat16
    )


def column_matrix(fine_count):
    return kernel_values(np.arange(fine_count)[:, None] - DECIM * np.arange(fine_count // DECIM)[None, :])


def dot(spec, a, b):
    return jnp.einsum(spec, a, b, preferred_element_type=jnp.float32)


def shards(latent, basis, response, hyper_obs, multi_obs):
    bf16 = jnp.bfloat16
    f32 = jnp.float32
    group = hyper_obs.shape[0]
    coarse = hyper_obs.shape[1]
    rows_dev = coarse * DECIM
    count = lax.axis_size("tile")
    up = [(i + 1, i) for i in range(count - 1)]
    down = [(i, i + 1) for i in range(count - 1)]
    cols = column_matrix(latent.shape[2])
    rows = kernel_values(
        np.arange(rows_dev)[:, None] - DECIM * (np.arange(coarse + 2 * RIM)[None, :] - RIM)
    )
    cols = jnp.asarray(cols)
    rows = jnp.asarray(rows)

    narrow = dot("qrc,cj->qrj", latent, cols).astype(bf16)
    narrow = lax.all_to_all(narrow, "spec", split_axis=0, concat_axis=1, tiled=True)
    part = dot("ri,qrj->qij", rows, narrow)
    above = lax.ppermute(part[:, :RIM].astype(bf16), "tile", up)
    below = lax.ppermute(part[:, RIM + coarse :].astype(bf16), "tile", down)
    own = part[:, RIM : RIM + coarse]
    zeros = jnp.zeros((own.shape[0], coarse - RIM, own.shape[2]), f32)
    own = (
        own
        + jnp.concatenate([below.astype(f32), zeros], axis=1)
        + jnp.concatenate([zeros, above.astype(f32)], axis=1)
    ).astype(bf16)
    blurred = lax.all_gather(own, "spec", axis=0, tiled=True)
    mine = lax.dynamic_slice_in_dim(basis, lax.axis_index("spec") * group, group, 0)
    hs_residual = (dot("bq,qij->bij", mine, blurred) - hyper_obs.astype(f32)).astype(bf16)
    back = dot("bq,bij->qij", mine, hs_residual).astype(bf16)
    back = lax.all_to_all(back, "spec", split_axis=0, concat_axis=0, tiled=True)
    back = back.reshape((lax.axis_size("spec"), -1) + back.shape[1:])
    back = jnp.sum(back.astype(f32), axis=0).astype(bf16)
    from_below = lax.ppermute(back[:, :RIM], "tile", up)
    from_above = lax.ppermute(back[:, coarse - RIM :], "tile", down)
    padded = jnp.concatenate([from_above, back, from_below], axis=1)
    rows_back = dot("ri,qij->qrj", rows, padded).astype(bf16)
    rows_back = lax.all_to_all(rows_back, "spec", split_axis=1, concat_axis=0, tiled=True)
    spread = dot("qrj,cj->qrc", rows_back, cols)
    mixed = dot("mb,bq->mq", response, basis).astype(bf16)
    multi_resid = (dot("mq,qrc->mrc", mixed, latent) - multi_obs.astype(f32)).astype(bf16)
    gradient = spread + dot("mq,mrc->qrc", mixed, multi_resid)
    z_next = (latent.astype(f32) - STEP * gradient).astype(bf16)
    return (z_next, hs_residual)


def solution(mesh):
    in_specs = (
        P(None, ("tile", "spec"), None),
        P(),
        P(),
        P("spec", "tile", None),
        P(None, ("tile", "spec"), None),
    )
    out_specs = (P(None, ("tile", "spec"), None), P("spec", "tile", None))
    return jax.shard_map(shards, mesh=mesh, in_specs=in_specs, out_specs=out_specs, check_vma=False)
```

```python
import jax
import jax.numpy as jnp
import numpy as np
from jax import lax
from jax.experimental import pallas as pl
from jax.experimental.pallas import tpu as pltpu
from jax.sharding import PartitionSpec as P

DECIM = 4
HALO = 128
RIM = HALO // DECIM
STEP = 0.3


def profile(where_at):
    narrow = np.float32(DECIM / 2.0)
    decay_len = np.float32(3.0 * HALO / 8.0)
    ripple = np.cos(where_at * np.float32(np.pi / 7.0))
    return np.exp(-where_at * where_at / (np.float32(2.0) * narrow * narrow)) + np.float32(
        0.5
    ) * np.exp(-np.abs(where_at) / decay_len) * ripple * ripple


def kernel_values(offsets):
    every_offset = np.arange(-HALO, HALO + 1).astype(np.float32)
    energy = np.sqrt(np.sum(profile(every_offset) ** 2))
    inside = np.abs(offsets) <= HALO
    return np.where(inside, profile(offsets.astype(np.float32)) / energy, np.float32(0.0)).astype(
        jnp.bfloat16
    )


def column_matrix(fine_count):
    return kernel_values(np.arange(fine_count)[:, None] - DECIM * np.arange(fine_count // DECIM)[None, :])


def dot(spec, a, b):
    return jnp.einsum(spec, a, b, preferred_element_type=jnp.float32)


def shards_plain(latent, basis, response, hyper_obs, multi_obs):
    bf16 = jnp.bfloat16
    f32 = jnp.float32
    group = hyper_obs.shape[0]
    coarse = hyper_obs.shape[1]
    rows_dev = coarse * DECIM
    count = lax.axis_size("tile")
    up = [(i + 1, i) for i in range(count - 1)]
    down = [(i, i + 1) for i in range(count - 1)]
    cols = column_matrix(latent.shape[2])
    rows = kernel_values(
        np.arange(rows_dev)[:, None] - DECIM * (np.arange(coarse + 2 * RIM)[None, :] - RIM)
    )
    cols = jnp.asarray(cols)
    rows = jnp.asarray(rows)

    narrow = dot("qrc,cj->qrj", latent, cols).astype(bf16)
    narrow = lax.all_to_all(narrow, "spec", split_axis=0, concat_axis=1, tiled=True)
    part = dot("ri,qrj->qij", rows, narrow)
    above = lax.ppermute(part[:, :RIM].astype(bf16), "tile", up)
    below = lax.ppermute(part[:, RIM + coarse :].astype(bf16), "tile", down)
    own = part[:, RIM : RIM + coarse]
    zeros = jnp.zeros((own.shape[0], coarse - RIM, own.shape[2]), f32)
    own = (
        own
        + jnp.concatenate([below.astype(f32), zeros], axis=1)
        + jnp.concatenate([zeros, above.astype(f32)], axis=1)
    ).astype(bf16)
    blurred = lax.all_gather(own, "spec", axis=0, tiled=True)
    mine = lax.dynamic_slice_in_dim(basis, lax.axis_index("spec") * group, group, 0)
    hs_residual = (dot("bq,qij->bij", mine, blurred) - hyper_obs.astype(f32)).astype(bf16)
    back = dot("bq,bij->qij", mine, hs_residual).astype(bf16)
    back = lax.all_to_all(back, "spec", split_axis=0, concat_axis=0, tiled=True)
    back = back.reshape((lax.axis_size("spec"), -1) + back.shape[1:])
    back = jnp.sum(back.astype(f32), axis=0).astype(bf16)
    from_below = lax.ppermute(back[:, :RIM], "tile", up)
    from_above = lax.ppermute(back[:, coarse - RIM :], "tile", down)
    padded = jnp.concatenate([from_above, back, from_below], axis=1)
    rows_back = dot("ri,qij->qrj", rows, padded).astype(bf16)
    rows_back = lax.all_to_all(rows_back, "spec", split_axis=1, concat_axis=0, tiled=True)
    spread = dot("qrj,cj->qrc", rows_back, cols)
    mixed = dot("mb,bq->mq", response, basis).astype(bf16)
    multi_resid = (dot("mq,qrc->mrc", mixed, latent) - multi_obs.astype(f32)).astype(bf16)
    gradient = spread + dot("mq,mrc->qrc", mixed, multi_resid)
    z_next = (latent.astype(f32) - STEP * gradient).astype(bf16)
    return (z_next, hs_residual)


N_SPEC = 4
SLAB = 64
WINDOW = 96
LANES = 128
MESH = pl.DeviceIdType.MESH
bf16 = jnp.bfloat16
f32 = jnp.float32


def mm(a, b):
    return jnp.dot(a, b, preferred_element_type=f32)


def mm_nt(a, b):
    return lax.dot_general(a, b, (((1,), (1,)), ((), ())), preferred_element_type=f32)


def same(shape, row_of, col_of):
    rows = row_of(lax.broadcasted_iota(jnp.int32, shape, 0))
    cols = col_of(lax.broadcasted_iota(jnp.int32, shape, 1))
    return jnp.where(rows == cols, 1.0, 0.0)


def low(i):
    return i & 15


def high(i):
    return i >> 4


def plain(i):
    return i


def joined(
    lat_hbm, mo_hbm, hy_hbm, basis, repeated, kc, kct, kri, krt,
    z_hbm, hs_hbm,
    lat, mo, hy, z, hs, base, msr, kb, kbt, km, kmt,
    s_a, r_a, own, s_h, r_h, s_x, r_x, blur, s_b, r_b, own_b, s_y, r_y, wide,
    in_sem, out_sem, send_sem, recv_sem,
):
    t = lax.axis_index("tile")
    s = lax.axis_index("spec")
    count = lax.axis_size("tile")
    x, core = s // 2, s % 2
    half = lat.shape[0] // 2
    partner = (t, 2 * x + 1 - core)
    peer = (t, 2 * (1 - x) + core)
    fwd, bwd = t - 1 + 2 * x, t + 1 - 2 * x
    has_fwd = jnp.logical_and(fwd >= 0, fwd < count)
    has_bwd = jnp.logical_and(bwd >= 0, bwd < count)
    mine = pl.multiple_of(half * core, half)
    other = pl.multiple_of(half * (1 - core), half)
    edge = pl.multiple_of(64 * x, 32)
    far = pl.multiple_of(64 * (1 - x), 32)
    tile0 = pl.multiple_of(32 * (1 - x), 32)
    part0 = pl.multiple_of(32 * x, 32)
    part1 = pl.multiple_of(32 * (1 - x), 32)

    loads = [
        pltpu.make_async_copy(
            lat_hbm.at[pl.ds(other, half)], lat.at[pl.ds(other, half)], in_sem.at[0]
        ),
        pltpu.make_async_copy(
            lat_hbm.at[pl.ds(mine, half)], lat.at[pl.ds(mine, half)], in_sem.at[1]
        ),
        pltpu.make_async_copy(mo_hbm, mo, in_sem.at[2]),
        pltpu.make_async_copy(hy_hbm, hy, in_sem.at[3]),
    ]
    for load in loads:
        load.start()

    barrier = pltpu.get_barrier_semaphore()
    pl.semaphore_signal(barrier, inc=1, device_id=partner, device_id_type=MESH)
    pl.semaphore_signal(barrier, inc=1, device_id=peer, device_id_type=MESH)

    @pl.when(has_fwd)
    def _():
        pl.semaphore_signal(barrier, inc=1, device_id=(fwd, s), device_id_type=MESH)

    @pl.when(has_bwd)
    def _():
        pl.semaphore_signal(barrier, inc=1, device_id=(bwd, s), device_id_type=MESH)

    def remote(kind, c, src, dst, device):
        return pltpu.make_async_remote_copy(
            src_ref=src,
            dst_ref=dst,
            send_sem=send_sem.at[kind, c],
            recv_sem=recv_sem.at[kind, c],
            device_id=device,
            device_id_type=MESH,
        )

    def both(c):
        return slice(c * LANES, (c + 1) * LANES)

    copy_a = [remote(0, c, s_a.at[c], r_a.at[c], partner) for c in range(2)]
    copy_h = [remote(1, c, s_h.at[c], r_h.at[c], (fwd, s)) for c in range(2)]
    copy_x0 = [remote(2, c, s_x.at[c, 0], r_x.at[c, 0], peer) for c in range(2)]
    copy_x1 = [remote(3, c, s_x.at[c, 1], r_x.at[c, 1], peer) for c in range(2)]
    copy_c = [remote(4, c, blur.at[c, core], blur.at[c, core], partner) for c in range(2)]
    copy_b = [remote(5, c, s_b.at[c], r_b.at[c], partner) for c in range(2)]
    copy_y0 = [remote(6, c, s_y.at[c, 0], r_y.at[c, 0], peer) for c in range(2)]
    copy_y1 = [remote(7, c, s_y.at[c, 1], r_y.at[c, 1], peer) for c in range(2)]
    copy_g = [
        remote(
            8, c, wide.at[c, core, :, pl.ds(far, 32)], wide.at[c, core, :, pl.ds(edge, 32)], (bwd, s)
        )
        for c in range(2)
    ]
    copy_d = [
        remote(
            9, c, wide.at[c, core, :, pl.ds(tile0, 64)], wide.at[c, core, :, pl.ds(tile0, 64)], partner
        )
        for c in range(2)
    ]
    copy_e = [
        remote(
            10, c, wide.at[c, core, :, pl.ds(edge, 32)], wide.at[c, core, :, pl.ds(edge, 32)], partner
        )
        for c in range(2)
    ]

    def partial(first, g):
        cells = lat[pl.ds(first + 4 * g, 4)].reshape(4 * SLAB, -1)
        narrow = mm(cells, kc[...]).astype(bf16)
        return mm(kri[core], narrow).reshape(4, WINDOW, 2 * LANES)

    loads[0].wait()

    @pl.loop(0, half // 4)
    def _(g):
        part = partial(other, g).astype(bf16)
        for c in range(2):
            s_a[c, pl.ds(4 * g, 4)] = part[:, :, both(c)]

    pl.semaphore_wait(barrier, 2 + has_fwd.astype(jnp.int32) + has_bwd.astype(jnp.int32))
    for c in range(2):
        copy_a[c].start()
    loads[1].wait()

    @pl.loop(0, half // 4)
    def _(g):
        part = partial(mine, g)
        for c in range(2):
            own[c, pl.ds(4 * g, 4)] = part[:, :, both(c)]

    for c in range(2):
        copy_a[c].wait_recv()
        s_h[c] = (own[c, :, pl.ds(edge, 32)] + r_a[c, :, pl.ds(edge, 32)].astype(f32)).astype(bf16)

        @pl.when(has_fwd)
        def _():
            copy_h[c].start()

        mid = own[c, :, 32:64] + r_a[c, :, 32:64].astype(f32)
        own[c, :, 32:64] = mid
        s_x[c, 0] = mid.astype(bf16)
        copy_x0[c].start()
        own[c, :, pl.ds(far, 32)] = own[c, :, pl.ds(far, 32)] + r_a[c, :, pl.ds(far, 32)].astype(f32)

    bands = hy.shape[0]
    lead = lat.shape[0] * 16
    spread_q = same((lat.shape[0], lead), plain, high).astype(bf16)
    spread_qt = same((lead, lat.shape[0]), high, plain).astype(bf16)
    pick = same((bands * 16, basis.shape[0]), lambda i: (i >> 4) + bands * s, plain).astype(bf16)
    pick_t = same((basis.shape[0], bands * 16), plain, lambda i: (i >> 4) + bands * s).astype(bf16)
    tall = mm_nt(spread_qt, basis[...]).astype(bf16)
    picked = mm(pick, basis[...]).astype(bf16)
    kb[...] = (mm(picked, spread_q) * same((bands * 16, lead), low, low)).astype(bf16)
    kbt[...] = (mm(tall, pick_t) * same((lead, bands * 16), low, low)).astype(bf16)
    mixed = mm(repeated[...], basis[...]).astype(bf16)
    km[...] = (mm(mixed, spread_q) * same((LANES, lead), low, low)).astype(bf16)
    kmt[...] = (mm_nt(tall, repeated[...]) * same((lead, LANES), low, low)).astype(bf16)

    for c in range(2):

        @pl.when(has_bwd)
        def _():
            copy_h[c].wait_recv()
            own[c, :, pl.ds(far, 32)] = own[c, :, pl.ds(far, 32)] + r_h[c].astype(f32)

        s_x[c, 1] = own[c, :, pl.ds(far, 32)].astype(bf16)
        copy_x1[c].start()

    loads[2].wait()

    @pl.loop(0, SLAB // 16)
    def _(g):
        at = pl.ds(pl.multiple_of(16 * g, 16), 16)
        for n in range(lat.shape[2] // 256):
            cut = slice(256 * n, 256 * n + 256)
            cells = lat[:, at, cut].reshape(lead, 256)
            resid = mm(km[...], cells) - mo[:, at, cut].reshape(LANES, 256).astype(f32)
            back = mm(kmt[...], resid.astype(bf16))
            base[:, at, cut] = (cells.astype(f32) - STEP * back).reshape(-1, 16, 256)

    for c in range(2):
        copy_x0[c].wait_recv()
        blur[c, core, :, pl.ds(part1, 32)] = (
            own[c, :, pl.ds(far, 32)] + r_x[c, 0].astype(f32)
        ).astype(bf16)
        copy_x1[c].wait_recv()
        blur[c, core, :, pl.ds(part0, 32)] = (own[c, :, 32:64] + r_x[c, 1].astype(f32)).astype(bf16)
        copy_c[c].start()

    loads[3].wait()
    stores = []
    for c in range(2):
        copy_c[c].wait()

        @pl.loop(0, SLAB // 16)
        def _(g):
            at = pl.ds(pl.multiple_of(16 * g, 16), 16)
            cells = blur[c, :, :, at].reshape(lead, LANES)
            resid = mm(kb[...], cells) - hy[:, at, both(c)].reshape(bands * 16, LANES).astype(f32)
            resid = resid.astype(bf16)
            hs[:, at, both(c)] = resid.reshape(bands, 16, LANES)
            given = mm(kbt[pl.ds(16 * other, 16 * half)], resid)
            s_b[c, :, at] = given.astype(bf16).reshape(half, 16, LANES)
            kept = mm(kbt[pl.ds(16 * mine, 16 * half)], resid)
            own_b[c, :, at] = kept.reshape(half, 16, LANES)

        copy_b[c].start()

    stores.append(pltpu.make_async_copy(hs, hs_hbm, out_sem.at[8]))
    stores[0].start()

    for c in range(2):
        copy_b[c].wait_recv()
        total = own_b[c] + r_b[c].astype(f32)
        own_b[c] = total
        s_y[c, 0] = own_b[c, :, pl.ds(part0, 32)].astype(bf16)
        copy_y0[c].start()
        s_y[c, 1] = own_b[c, :, pl.ds(part1, 32)].astype(bf16)
        copy_y1[c].start()

    for c in range(2):
        copy_y0[c].wait_recv()
        wide[c, core, :, pl.ds(far, 32)] = (
            own_b[c, :, pl.ds(part1, 32)] + r_y[c, 0].astype(f32)
        ).astype(bf16)

        @pl.when(has_bwd)
        def _():
            copy_g[c].start()

        copy_y1[c].wait_recv()
        wide[c, core, :, 32:64] = (own_b[c, :, pl.ds(part0, 32)] + r_y[c, 1].astype(f32)).astype(bf16)
        copy_d[c].start()

    for c in range(2):

        @pl.when(has_fwd)
        def _():
            copy_g[c].wait_recv()

        @pl.when(jnp.logical_not(has_fwd))
        def _():
            wide[c, core, :, pl.ds(edge, 32)] = jnp.zeros((half, 32, LANES), bf16)

        copy_e[c].start()

    def finish(first, who, slot):
        def group(g, carry):
            cells = jnp.concatenate(
                [wide[c, who, pl.ds(4 * g, 4)].reshape(4 * WINDOW, LANES) for c in range(2)], axis=1
            )
            rows = mm(krt[core], cells).astype(bf16)
            at = pl.ds(first + 4 * g, 4)
            for n in range(lat.shape[2] // 256):
                cut = slice(256 * n, 256 * n + 256)
                back = mm(rows, kct[:, cut]).reshape(4, SLAB, 256)
                z[at, :, cut] = (base[at, :, cut] - STEP * back).astype(bf16)
            return carry

        lax.fori_loop(0, half // 4, group, 0)
        store = pltpu.make_async_copy(
            z.at[pl.ds(first, half)], z_hbm.at[pl.ds(first, half)], out_sem.at[slot]
        )
        store.start()
        stores.append(store)

    finish(mine, core, 0)
    for c in range(2):
        copy_d[c].wait_recv()
        copy_e[c].wait_recv()
    finish(other, 1 - core, 1)

    for c in range(2):
        for copies in (copy_a, copy_x0, copy_x1, copy_b, copy_y0, copy_y1, copy_d, copy_e):
            copies[c].wait_send()

        @pl.when(has_fwd)
        def _():
            copy_h[c].wait_send()

        @pl.when(has_bwd)
        def _():
            copy_g[c].wait_send()

    for store in stores:
        store.wait()


def row_window(core):
    return kernel_values(
        SLAB * core + np.arange(SLAB)[None, :] - DECIM * np.arange(WINDOW)[:, None] + HALO
    )


def shards_joined(latent, basis, response, hyper_obs, multi_obs):
    cols = column_matrix(latent.shape[2])
    row = np.stack([np.kron(np.eye(4, dtype=np.float32), row_window(c).astype(np.float32)) for c in (0, 1)])
    row = row.astype(bf16)
    lead = latent.shape[0] * 16
    bands = hyper_obs.shape[0] * 16
    half = latent.shape[0] // 2
    coarse, low_cols = hyper_obs.shape[1:]

    def buf(shape, dtype=bf16):
        return pltpu.VMEM(shape, dtype)

    any_spec = pl.BlockSpec(memory_space=pl.ANY)
    vmem_spec = pl.BlockSpec(memory_space=pltpu.VMEM)
    return pl.pallas_call(
        joined,
        out_shape=(
            jax.ShapeDtypeStruct(latent.shape, bf16),
            jax.ShapeDtypeStruct(hyper_obs.shape, bf16),
        ),
        in_specs=[any_spec] * 3 + [vmem_spec] * 6,
        out_specs=(any_spec, any_spec),
        scratch_shapes=[
            buf(latent.shape),
            buf(multi_obs.shape),
            buf(hyper_obs.shape),
            buf(latent.shape),
            buf(hyper_obs.shape),
            buf(latent.shape, f32),
            buf((8, LANES)),
            buf((bands, lead)),
            buf((lead, bands)),
            buf((LANES, lead)),
            buf((lead, LANES)),
            buf((2, half, WINDOW, LANES)),
            buf((2, half, WINDOW, LANES)),
            buf((2, half, WINDOW, LANES), f32),
            buf((2, half, 32, LANES)),
            buf((2, half, 32, LANES)),
            buf((2, 2, half, 32, LANES)),
            buf((2, 2, half, 32, LANES)),
            buf((2, 2, half, coarse, LANES)),
            buf((2, half, coarse, LANES)),
            buf((2, half, coarse, LANES)),
            buf((2, half, coarse, LANES), f32),
            buf((2, 2, half, 32, LANES)),
            buf((2, 2, half, 32, LANES)),
            buf((2, 2, half, WINDOW, LANES)),
            pltpu.SemaphoreType.DMA((4,)),
            pltpu.SemaphoreType.DMA((9,)),
            pltpu.SemaphoreType.DMA((11, 2)),
            pltpu.SemaphoreType.DMA((11, 2)),
        ],
        compiler_params=pltpu.CompilerParams(
            collective_id=0, has_side_effects=True, vmem_limit_bytes=56 * 1024 * 1024
        ),
        cost_estimate=pl.CostEstimate(
            flops=10 * 1024**3, bytes_accessed=13 * 1024 * 1024, transcendentals=0
        ),
        name="joined",
    )(
        latent,
        multi_obs,
        hyper_obs,
        basis,
        jnp.repeat(response, 16, axis=0),
        jnp.asarray(cols),
        jnp.asarray(cols.T),
        jnp.asarray(row),
        jnp.asarray(row.transpose(0, 2, 1)),
    )


def shards(latent, basis, response, hyper_obs, multi_obs):
    fits = (
        lax.axis_size("spec") == N_SPEC
        and latent.shape == (32, SLAB, 1024)
        and hyper_obs.shape[1:] == (SLAB, 2 * LANES)
    )
    run = shards_joined if fits else shards_plain
    return run(latent, basis, response, hyper_obs, multi_obs)


def solution(mesh):
    in_specs = (
        P(None, ("tile", "spec"), None),
        P(),
        P(),
        P("spec", "tile", None),
        P(None, ("tile", "spec"), None),
    )
    out_specs = (P(None, ("tile", "spec"), None), P("spec", "tile", None))
    return jax.shard_map(shards, mesh=mesh, in_specs=in_specs, out_specs=out_specs, check_vma=False)
```

```python
import jax
import jax.numpy as jnp
import numpy as np
from jax import lax
from jax.experimental import pallas as pl
from jax.experimental.pallas import tpu as pltpu
from jax.sharding import PartitionSpec as P

DECIM = 4
HALO = 128
RIM = HALO // DECIM
STEP = 0.3


def profile(where_at):
    narrow = np.float32(DECIM / 2.0)
    decay_len = np.float32(3.0 * HALO / 8.0)
    ripple = np.cos(where_at * np.float32(np.pi / 7.0))
    return np.exp(-where_at * where_at / (np.float32(2.0) * narrow * narrow)) + np.float32(
        0.5
    ) * np.exp(-np.abs(where_at) / decay_len) * ripple * ripple


def kernel_values(offsets):
    every_offset = np.arange(-HALO, HALO + 1).astype(np.float32)
    energy = np.sqrt(np.sum(profile(every_offset) ** 2))
    inside = np.abs(offsets) <= HALO
    return np.where(inside, profile(offsets.astype(np.float32)) / energy, np.float32(0.0)).astype(
        jnp.bfloat16
    )


def column_matrix(fine_count):
    return kernel_values(np.arange(fine_count)[:, None] - DECIM * np.arange(fine_count // DECIM)[None, :])


def dot(spec, a, b):
    return jnp.einsum(spec, a, b, preferred_element_type=jnp.float32)


def shards_plain(latent, basis, response, hyper_obs, multi_obs):
    bf16 = jnp.bfloat16
    f32 = jnp.float32
    group = hyper_obs.shape[0]
    coarse = hyper_obs.shape[1]
    rows_dev = coarse * DECIM
    count = lax.axis_size("tile")
    up = [(i + 1, i) for i in range(count - 1)]
    down = [(i, i + 1) for i in range(count - 1)]
    cols = column_matrix(latent.shape[2])
    rows = kernel_values(
        np.arange(rows_dev)[:, None] - DECIM * (np.arange(coarse + 2 * RIM)[None, :] - RIM)
    )
    cols = jnp.asarray(cols)
    rows = jnp.asarray(rows)

    narrow = dot("qrc,cj->qrj", latent, cols).astype(bf16)
    narrow = lax.all_to_all(narrow, "spec", split_axis=0, concat_axis=1, tiled=True)
    part = dot("ri,qrj->qij", rows, narrow)
    above = lax.ppermute(part[:, :RIM].astype(bf16), "tile", up)
    below = lax.ppermute(part[:, RIM + coarse :].astype(bf16), "tile", down)
    own = part[:, RIM : RIM + coarse]
    zeros = jnp.zeros((own.shape[0], coarse - RIM, own.shape[2]), f32)
    own = (
        own
        + jnp.concatenate([below.astype(f32), zeros], axis=1)
        + jnp.concatenate([zeros, above.astype(f32)], axis=1)
    ).astype(bf16)
    blurred = lax.all_gather(own, "spec", axis=0, tiled=True)
    mine = lax.dynamic_slice_in_dim(basis, lax.axis_index("spec") * group, group, 0)
    hs_residual = (dot("bq,qij->bij", mine, blurred) - hyper_obs.astype(f32)).astype(bf16)
    back = dot("bq,bij->qij", mine, hs_residual).astype(bf16)
    back = lax.all_to_all(back, "spec", split_axis=0, concat_axis=0, tiled=True)
    back = back.reshape((lax.axis_size("spec"), -1) + back.shape[1:])
    back = jnp.sum(back.astype(f32), axis=0).astype(bf16)
    from_below = lax.ppermute(back[:, :RIM], "tile", up)
    from_above = lax.ppermute(back[:, coarse - RIM :], "tile", down)
    padded = jnp.concatenate([from_above, back, from_below], axis=1)
    rows_back = dot("ri,qij->qrj", rows, padded).astype(bf16)
    rows_back = lax.all_to_all(rows_back, "spec", split_axis=1, concat_axis=0, tiled=True)
    spread = dot("qrj,cj->qrc", rows_back, cols)
    mixed = dot("mb,bq->mq", response, basis).astype(bf16)
    multi_resid = (dot("mq,qrc->mrc", mixed, latent) - multi_obs.astype(f32)).astype(bf16)
    gradient = spread + dot("mq,mrc->qrc", mixed, multi_resid)
    z_next = (latent.astype(f32) - STEP * gradient).astype(bf16)
    return (z_next, hs_residual)


N_SPEC = 4
SLAB = 64
WINDOW = 96
LANES = 128
MESH = pl.DeviceIdType.MESH
bf16 = jnp.bfloat16
f32 = jnp.float32


def mm(a, b):
    return jnp.dot(a, b, preferred_element_type=f32)


def mm_nt(a, b):
    return lax.dot_general(a, b, (((1,), (1,)), ((), ())), preferred_element_type=f32)


def same(shape, row_of, col_of):
    rows = row_of(lax.broadcasted_iota(jnp.int32, shape, 0))
    cols = col_of(lax.broadcasted_iota(jnp.int32, shape, 1))
    return jnp.where(rows == cols, 1.0, 0.0)


def low(i):
    return i & 15


def high(i):
    return i >> 4


def plain(i):
    return i


def joined(
    lat_hbm, mo_hbm, hy_hbm, basis_t, response, kc, kct, kri, krt,
    z_hbm, hs_hbm,
    lat, mo, hy, z, hs, base, kb, kbt, km, kmt, ks,
    s_a, r_a, own, s_h, r_h, s_x, r_x, blur, s_b, r_b, own_b, s_y, r_y, wide,
    in_sem, out_sem, send_sem, recv_sem,
):
    t = lax.axis_index("tile")
    s = lax.axis_index("spec")
    count = lax.axis_size("tile")
    x, core = s // 2, s % 2
    half = lat.shape[0] // 2
    partner = (t, 2 * x + 1 - core)
    peer = (t, 2 * (1 - x) + core)
    fwd, bwd = t - 1 + 2 * x, t + 1 - 2 * x
    has_fwd = jnp.logical_and(fwd >= 0, fwd < count)
    has_bwd = jnp.logical_and(bwd >= 0, bwd < count)
    mine = pl.multiple_of(half * core, half)
    other = pl.multiple_of(half * (1 - core), half)
    edge = pl.multiple_of(64 * x, 32)
    far = pl.multiple_of(64 * (1 - x), 32)
    tile0 = pl.multiple_of(32 * (1 - x), 32)
    part0 = pl.multiple_of(32 * x, 32)
    part1 = pl.multiple_of(32 * (1 - x), 32)

    loads = [
        pltpu.make_async_copy(
            lat_hbm.at[pl.ds(other, half)], lat.at[pl.ds(other, half)], in_sem.at[0]
        ),
        pltpu.make_async_copy(
            lat_hbm.at[pl.ds(mine, half)], lat.at[pl.ds(mine, half)], in_sem.at[1]
        ),
        pltpu.make_async_copy(mo_hbm, mo, in_sem.at[2]),
        pltpu.make_async_copy(hy_hbm, hy, in_sem.at[3]),
    ]
    for load in (loads[3], loads[0], loads[1], loads[2]):
        load.start()

    barrier = pltpu.get_barrier_semaphore()
    pl.semaphore_signal(barrier, inc=1, device_id=partner, device_id_type=MESH)
    pl.semaphore_signal(barrier, inc=1, device_id=peer, device_id_type=MESH)

    @pl.when(has_fwd)
    def _():
        pl.semaphore_signal(barrier, inc=1, device_id=(fwd, s), device_id_type=MESH)

    @pl.when(has_bwd)
    def _():
        pl.semaphore_signal(barrier, inc=1, device_id=(bwd, s), device_id_type=MESH)

    def remote(kind, c, src, dst, device):
        return pltpu.make_async_remote_copy(
            src_ref=src,
            dst_ref=dst,
            send_sem=send_sem.at[kind, c],
            recv_sem=recv_sem.at[kind, c],
            device_id=device,
            device_id_type=MESH,
        )

    def both(c):
        return slice(c * LANES, (c + 1) * LANES)

    copy_a = [remote(0, c, s_a.at[c], r_a.at[c], partner) for c in range(2)]
    copy_h = [remote(1, c, s_h.at[c], r_h.at[c], (fwd, s)) for c in range(2)]
    copy_x0 = [remote(2, c, s_x.at[c, 0], r_x.at[c, 0], peer) for c in range(2)]
    copy_x1 = [remote(3, c, s_x.at[c, 1], r_x.at[c, 1], peer) for c in range(2)]
    copy_c = [remote(4, c, blur.at[c, core], blur.at[c, core], partner) for c in range(2)]
    copy_b = [remote(5, c, s_b.at[c], r_b.at[c], partner) for c in range(2)]
    copy_y = [remote(6, c, s_y.at[c], r_y.at[c], peer) for c in range(2)]
    copy_g = [
        remote(
            7, c, wide.at[c, core, :, pl.ds(far, 32)], wide.at[c, core, :, pl.ds(edge, 32)], (bwd, s)
        )
        for c in range(2)
    ]
    copy_d = [
        remote(
            8, c, wide.at[c, core, :, pl.ds(tile0, 64)], wide.at[c, core, :, pl.ds(tile0, 64)], partner
        )
        for c in range(2)
    ]
    copy_e = [
        remote(
            9, c, wide.at[c, core, :, pl.ds(edge, 32)], wide.at[c, core, :, pl.ds(edge, 32)], partner
        )
        for c in range(2)
    ]

    def partial(first, g):
        cells = lat[pl.ds(first + 4 * g, 4)].reshape(4 * SLAB, -1)
        narrow = mm(cells, kc[...]).astype(bf16)
        return mm(kri[core], narrow).reshape(4, WINDOW, 2 * LANES)

    bands = hy.shape[0]
    lead = lat.shape[0] * 16
    all_bands = basis_t.shape[1]
    spread_q = same((lat.shape[0], lead), plain, high).astype(bf16)
    spread_qt = same((lead, lat.shape[0]), high, plain).astype(bf16)
    tall = mm(spread_qt, basis_t[...]).astype(bf16)
    pick_t = same((all_bands, bands * 16), plain, lambda i: (i >> 4) + bands * s).astype(bf16)
    kbt[...] = (mm(tall, pick_t) * same((lead, bands * 16), low, low)).astype(bf16)

    loads[3].wait()

    def observed(at, width):
        return hy[:, at, width].reshape(bands * 16, -1)

    @pl.loop(0, SLAB // 16)
    def _(g):
        at = pl.ds(pl.multiple_of(16 * g, 16), 16)
        given = mm(kbt[pl.ds(16 * other, 16 * half)], observed(at, slice(None)))
        given = given.astype(bf16).reshape(half, 16, 2 * LANES)
        for c in range(2):
            s_b[c, :, at] = given[:, :, both(c)]

    pl.semaphore_wait(barrier, 2 + has_fwd.astype(jnp.int32) + has_bwd.astype(jnp.int32))
    for c in range(2):
        copy_b[c].start()

    loads[0].wait()

    @pl.loop(0, half // 4)
    def _(g):
        part = partial(other, g).astype(bf16)
        for c in range(2):
            s_a[c, pl.ds(4 * g, 4)] = part[:, :, both(c)]

    for c in range(2):
        copy_a[c].start()

    @pl.loop(0, SLAB // 16)
    def _(g):
        at = pl.ds(pl.multiple_of(16 * g, 16), 16)
        kept = mm(kbt[pl.ds(16 * mine, 16 * half)], observed(at, slice(None)))
        kept = kept.reshape(half, 16, 2 * LANES)
        for c in range(2):
            own_b[c, :, at] = kept[:, :, both(c)]

    def share(c):
        copy_b[c].wait_recv()
        total = own_b[c] + r_b[c].astype(f32)
        own_b[c] = total
        s_y[c] = total.astype(bf16)
        copy_y[c].start()

    share(0)
    loads[1].wait()

    @pl.loop(0, half // 4)
    def _(g):
        part = partial(mine, g)
        for c in range(2):
            own[c, pl.ds(4 * g, 4)] = part[:, :, both(c)]

    for c in range(2):
        copy_a[c].wait_recv()
        s_h[c] = (own[c, :, pl.ds(edge, 32)] + r_a[c, :, pl.ds(edge, 32)].astype(f32)).astype(bf16)

        @pl.when(has_fwd)
        def _():
            copy_h[c].start()

        mid = own[c, :, 32:64] + r_a[c, :, 32:64].astype(f32)
        own[c, :, 32:64] = mid
        s_x[c, 0] = mid.astype(bf16)
        copy_x0[c].start()
        own[c, :, pl.ds(far, 32)] = own[c, :, pl.ds(far, 32)] + r_a[c, :, pl.ds(far, 32)].astype(f32)

    pick = same((bands * 16, all_bands), lambda i: (i >> 4) + bands * s, plain).astype(bf16)
    repeated = jnp.broadcast_to(
        response[...].astype(f32)[:, None, :], (response.shape[0], 16, all_bands)
    )
    repeated = repeated.reshape(LANES, all_bands).astype(bf16)
    picked = mm_nt(pick, basis_t[...]).astype(bf16)
    kb[...] = (mm(picked, spread_q) * same((bands * 16, lead), low, low)).astype(bf16)
    mixed = mm_nt(repeated, basis_t[...]).astype(bf16)
    km[...] = (mm(mixed, spread_q) * same((LANES, lead), low, low)).astype(bf16)
    kmt[...] = (mm_nt(tall, repeated) * same((lead, LANES), low, low)).astype(bf16)
    square = mm_nt(basis_t[...], basis_t[...])
    first = square.astype(bf16)
    second = (square - first.astype(f32)).astype(bf16)
    for k, part in enumerate((first, second)):
        grown = mm(mm(spread_qt, part).astype(bf16), spread_q)
        ks[k] = (grown * same((lead, lead), low, low)).astype(bf16)

    for c in range(2):

        @pl.when(has_bwd)
        def _():
            copy_h[c].wait_recv()
            own[c, :, pl.ds(far, 32)] = own[c, :, pl.ds(far, 32)] + r_h[c].astype(f32)

        s_x[c, 1] = own[c, :, pl.ds(far, 32)].astype(bf16)
        copy_x1[c].start()

    share(1)
    loads[2].wait()

    @pl.loop(0, SLAB // 16)
    def _(g):
        at = pl.ds(pl.multiple_of(16 * g, 16), 16)
        for n in range(lat.shape[2] // 256):
            cut = slice(256 * n, 256 * n + 256)
            cells = lat[:, at, cut].reshape(lead, 256)
            resid = mm(km[...], cells) - mo[:, at, cut].reshape(LANES, 256).astype(f32)
            back = mm(kmt[...], resid.astype(bf16))
            base[:, at, cut] = (cells.astype(f32) - STEP * back).reshape(-1, 16, 256)

    for c in range(2):
        copy_x0[c].wait_recv()
        blur[c, core, :, pl.ds(part1, 32)] = (
            own[c, :, pl.ds(far, 32)] + r_x[c, 0].astype(f32)
        ).astype(bf16)
        copy_x1[c].wait_recv()
        blur[c, core, :, pl.ds(part0, 32)] = (own[c, :, 32:64] + r_x[c, 1].astype(f32)).astype(bf16)
        copy_c[c].start()

    stores = []
    for c in range(2):
        copy_c[c].wait()
        copy_y[c].wait_recv()

        @pl.loop(0, SLAB // 16)
        def _(g):
            at = pl.ds(pl.multiple_of(16 * g, 16), 16)
            cells = blur[c, :, :, at].reshape(lead, LANES)
            rows = pl.ds(16 * mine, 16 * half)
            total = mm(ks[0, rows], cells) + mm(ks[1, rows], cells)
            total = total.reshape(half, 16, LANES) - own_b[c, :, at] - r_y[c, :, at].astype(f32)
            wide[c, core, :, pl.ds(pl.multiple_of(tile0 + 16 * g, 16), 16)] = total.astype(bf16)

        @pl.when(has_bwd)
        def _():
            copy_g[c].start()

        copy_d[c].start()

    @pl.loop(0, SLAB // 16)
    def _(g):
        at = pl.ds(pl.multiple_of(16 * g, 16), 16)
        cells = jnp.concatenate(
            [blur[c, :, :, at].reshape(lead, LANES) for c in range(2)], axis=1
        )
        resid = mm(kb[...], cells) - observed(at, slice(None)).astype(f32)
        hs[:, at] = resid.astype(bf16).reshape(bands, 16, 2 * LANES)

    stores.append(pltpu.make_async_copy(hs, hs_hbm, out_sem.at[8]))
    stores[0].start()

    for c in range(2):

        @pl.when(has_fwd)
        def _():
            copy_g[c].wait_recv()

        @pl.when(jnp.logical_not(has_fwd))
        def _():
            wide[c, core, :, pl.ds(edge, 32)] = jnp.zeros((half, 32, LANES), bf16)

        copy_e[c].start()

    def finish(first, who, slot):
        def group(g, carry):
            cells = jnp.concatenate(
                [wide[c, who, pl.ds(4 * g, 4)].reshape(4 * WINDOW, LANES) for c in range(2)], axis=1
            )
            rows = mm(krt[core], cells).astype(bf16)
            at = pl.ds(first + 4 * g, 4)
            for n in range(lat.shape[2] // 256):
                cut = slice(256 * n, 256 * n + 256)
                back = mm(rows, kct[:, cut]).reshape(4, SLAB, 256)
                z[at, :, cut] = (base[at, :, cut] - STEP * back).astype(bf16)
            return carry

        lax.fori_loop(0, half // 4, group, 0)
        store = pltpu.make_async_copy(
            z.at[pl.ds(first, half)], z_hbm.at[pl.ds(first, half)], out_sem.at[slot]
        )
        store.start()
        stores.append(store)

    finish(mine, core, 0)
    for c in range(2):
        copy_d[c].wait_recv()
        copy_e[c].wait_recv()
    finish(other, 1 - core, 1)

    for c in range(2):
        for copies in (copy_a, copy_x0, copy_x1, copy_b, copy_y, copy_d, copy_e):
            copies[c].wait_send()

        @pl.when(has_fwd)
        def _():
            copy_h[c].wait_send()

        @pl.when(has_bwd)
        def _():
            copy_g[c].wait_send()

    for store in stores:
        store.wait()


def row_window(core):
    return kernel_values(
        SLAB * core + np.arange(SLAB)[None, :] - DECIM * np.arange(WINDOW)[:, None] + HALO
    )


def shards_joined(latent, basis, response, hyper_obs, multi_obs):
    cols = column_matrix(latent.shape[2])
    row = np.stack([np.kron(np.eye(4, dtype=np.float32), row_window(c).astype(np.float32)) for c in (0, 1)])
    row = row.astype(bf16)
    lead = latent.shape[0] * 16
    bands = hyper_obs.shape[0] * 16
    half = latent.shape[0] // 2
    coarse, low_cols = hyper_obs.shape[1:]

    def buf(shape, dtype=bf16):
        return pltpu.VMEM(shape, dtype)

    any_spec = pl.BlockSpec(memory_space=pl.ANY)
    vmem_spec = pl.BlockSpec(memory_space=pltpu.VMEM)
    return pl.pallas_call(
        joined,
        out_shape=(
            jax.ShapeDtypeStruct(latent.shape, bf16),
            jax.ShapeDtypeStruct(hyper_obs.shape, bf16),
        ),
        in_specs=[any_spec] * 3 + [vmem_spec] * 6,
        out_specs=(any_spec, any_spec),
        scratch_shapes=[
            buf(latent.shape),
            buf(multi_obs.shape),
            buf(hyper_obs.shape),
            buf(latent.shape),
            buf(hyper_obs.shape),
            buf(latent.shape, f32),
            buf((bands, lead)),
            buf((lead, bands)),
            buf((LANES, lead)),
            buf((lead, LANES)),
            buf((2, lead, lead)),
            buf((2, half, WINDOW, LANES)),
            buf((2, half, WINDOW, LANES)),
            buf((2, half, WINDOW, LANES), f32),
            buf((2, half, 32, LANES)),
            buf((2, half, 32, LANES)),
            buf((2, 2, half, 32, LANES)),
            buf((2, 2, half, 32, LANES)),
            buf((2, 2, half, coarse, LANES)),
            buf((2, half, coarse, LANES)),
            buf((2, half, coarse, LANES)),
            buf((2, half, coarse, LANES), f32),
            buf((2, half, coarse, LANES)),
            buf((2, half, coarse, LANES)),
            buf((2, 2, half, WINDOW, LANES)),
            pltpu.SemaphoreType.DMA((4,)),
            pltpu.SemaphoreType.DMA((9,)),
            pltpu.SemaphoreType.DMA((10, 2)),
            pltpu.SemaphoreType.DMA((10, 2)),
        ],
        compiler_params=pltpu.CompilerParams(
            collective_id=0, has_side_effects=True, vmem_limit_bytes=56 * 1024 * 1024
        ),
        cost_estimate=pl.CostEstimate(
            flops=10 * 1024**3, bytes_accessed=13 * 1024 * 1024, transcendentals=0
        ),
        name="joined",
    )(
        latent,
        multi_obs,
        hyper_obs,
        basis.T,
        response,
        jnp.asarray(cols),
        jnp.asarray(cols.T),
        jnp.asarray(row),
        jnp.asarray(row.transpose(0, 2, 1)),
    )


def shards(latent, basis, response, hyper_obs, multi_obs):
    fits = (
        lax.axis_size("spec") == N_SPEC
        and latent.shape == (32, SLAB, 1024)
        and hyper_obs.shape[1:] == (SLAB, 2 * LANES)
    )
    run = shards_joined if fits else shards_plain
    return run(latent, basis, response, hyper_obs, multi_obs)


def solution(mesh):
    in_specs = (
        P(None, ("tile", "spec"), None),
        P(),
        P(),
        P("spec", "tile", None),
        P(None, ("tile", "spec"), None),
    )
    out_specs = (P(None, ("tile", "spec"), None), P("spec", "tile", None))
    return jax.shard_map(shards, mesh=mesh, in_specs=in_specs, out_specs=out_specs, check_vma=False)
```

```python
import jax
import jax.numpy as jnp
import numpy as np
from jax import lax
from jax.experimental import pallas as pl
from jax.experimental.pallas import tpu as pltpu
from jax.sharding import PartitionSpec as P

DECIM = 4
HALO = 128
RIM = HALO // DECIM
STEP = 0.3


def profile(where_at):
    narrow = np.float32(DECIM / 2.0)
    decay_len = np.float32(3.0 * HALO / 8.0)
    ripple = np.cos(where_at * np.float32(np.pi / 7.0))
    return np.exp(-where_at * where_at / (np.float32(2.0) * narrow * narrow)) + np.float32(
        0.5
    ) * np.exp(-np.abs(where_at) / decay_len) * ripple * ripple


def kernel_values(offsets):
    every_offset = np.arange(-HALO, HALO + 1).astype(np.float32)
    energy = np.sqrt(np.sum(profile(every_offset) ** 2))
    inside = np.abs(offsets) <= HALO
    return np.where(inside, profile(offsets.astype(np.float32)) / energy, np.float32(0.0)).astype(
        jnp.bfloat16
    )


def column_matrix(fine_count):
    return kernel_values(np.arange(fine_count)[:, None] - DECIM * np.arange(fine_count // DECIM)[None, :])


def dot(spec, a, b):
    return jnp.einsum(spec, a, b, preferred_element_type=jnp.float32)


def shards_plain(latent, basis, response, hyper_obs, multi_obs):
    bf16 = jnp.bfloat16
    f32 = jnp.float32
    group = hyper_obs.shape[0]
    coarse = hyper_obs.shape[1]
    rows_dev = coarse * DECIM
    count = lax.axis_size("tile")
    up = [(i + 1, i) for i in range(count - 1)]
    down = [(i, i + 1) for i in range(count - 1)]
    cols = column_matrix(latent.shape[2])
    rows = kernel_values(
        np.arange(rows_dev)[:, None] - DECIM * (np.arange(coarse + 2 * RIM)[None, :] - RIM)
    )
    cols = jnp.asarray(cols)
    rows = jnp.asarray(rows)

    narrow = dot("qrc,cj->qrj", latent, cols).astype(bf16)
    narrow = lax.all_to_all(narrow, "spec", split_axis=0, concat_axis=1, tiled=True)
    part = dot("ri,qrj->qij", rows, narrow)
    above = lax.ppermute(part[:, :RIM].astype(bf16), "tile", up)
    below = lax.ppermute(part[:, RIM + coarse :].astype(bf16), "tile", down)
    own = part[:, RIM : RIM + coarse]
    zeros = jnp.zeros((own.shape[0], coarse - RIM, own.shape[2]), f32)
    own = (
        own
        + jnp.concatenate([below.astype(f32), zeros], axis=1)
        + jnp.concatenate([zeros, above.astype(f32)], axis=1)
    ).astype(bf16)
    blurred = lax.all_gather(own, "spec", axis=0, tiled=True)
    mine = lax.dynamic_slice_in_dim(basis, lax.axis_index("spec") * group, group, 0)
    hs_residual = (dot("bq,qij->bij", mine, blurred) - hyper_obs.astype(f32)).astype(bf16)
    back = dot("bq,bij->qij", mine, hs_residual).astype(bf16)
    back = lax.all_to_all(back, "spec", split_axis=0, concat_axis=0, tiled=True)
    back = back.reshape((lax.axis_size("spec"), -1) + back.shape[1:])
    back = jnp.sum(back.astype(f32), axis=0).astype(bf16)
    from_below = lax.ppermute(back[:, :RIM], "tile", up)
    from_above = lax.ppermute(back[:, coarse - RIM :], "tile", down)
    padded = jnp.concatenate([from_above, back, from_below], axis=1)
    rows_back = dot("ri,qij->qrj", rows, padded).astype(bf16)
    rows_back = lax.all_to_all(rows_back, "spec", split_axis=1, concat_axis=0, tiled=True)
    spread = dot("qrj,cj->qrc", rows_back, cols)
    mixed = dot("mb,bq->mq", response, basis).astype(bf16)
    multi_resid = (dot("mq,qrc->mrc", mixed, latent) - multi_obs.astype(f32)).astype(bf16)
    gradient = spread + dot("mq,mrc->qrc", mixed, multi_resid)
    z_next = (latent.astype(f32) - STEP * gradient).astype(bf16)
    return (z_next, hs_residual)


N_SPEC = 4
SLAB = 64
WINDOW = 96
LANES = 128
MESH = pl.DeviceIdType.MESH
bf16 = jnp.bfloat16
f32 = jnp.float32


def mm(a, b):
    return jnp.dot(a, b, preferred_element_type=f32)


def mm_nt(a, b):
    return lax.dot_general(a, b, (((1,), (1,)), ((), ())), preferred_element_type=f32)


def same(shape, row_of, col_of):
    rows = row_of(lax.broadcasted_iota(jnp.int32, shape, 0))
    cols = col_of(lax.broadcasted_iota(jnp.int32, shape, 1))
    return jnp.where(rows == cols, 1.0, 0.0)


def low(i):
    return i & 15


def high(i):
    return i >> 4


def plain(i):
    return i


def joined(
    lat_hbm, mo_hbm, hy_hbm, basis_t, response, kc, kri, krt,
    sp_hbm, ms_hbm, kmt_hbm, hs_hbm,
    lat, mo, hy, sp, hs, msr, kb, kbt, km, kmt, ks,
    s_a, r_a, own, s_h, r_h, s_x, r_x, blur, s_b, r_b, own_b, s_y, r_y, wide,
    in_sem, out_sem, send_sem, recv_sem,
):
    t = lax.axis_index("tile")
    s = lax.axis_index("spec")
    count = lax.axis_size("tile")
    x, core = s // 2, s % 2
    half = lat.shape[0] // 2
    partner = (t, 2 * x + 1 - core)
    peer = (t, 2 * (1 - x) + core)
    fwd, bwd = t - 1 + 2 * x, t + 1 - 2 * x
    has_fwd = jnp.logical_and(fwd >= 0, fwd < count)
    has_bwd = jnp.logical_and(bwd >= 0, bwd < count)
    mine = pl.multiple_of(half * core, half)
    other = pl.multiple_of(half * (1 - core), half)
    edge = pl.multiple_of(64 * x, 32)
    far = pl.multiple_of(64 * (1 - x), 32)
    tile0 = pl.multiple_of(32 * (1 - x), 32)
    part0 = pl.multiple_of(32 * x, 32)
    part1 = pl.multiple_of(32 * (1 - x), 32)

    loads = [
        pltpu.make_async_copy(
            lat_hbm.at[pl.ds(other, half)], lat.at[pl.ds(other, half)], in_sem.at[0]
        ),
        pltpu.make_async_copy(
            lat_hbm.at[pl.ds(mine, half)], lat.at[pl.ds(mine, half)], in_sem.at[1]
        ),
        pltpu.make_async_copy(mo_hbm, mo, in_sem.at[2]),
        pltpu.make_async_copy(hy_hbm, hy, in_sem.at[3]),
    ]
    for load in (loads[3], loads[0], loads[1], loads[2]):
        load.start()

    barrier = pltpu.get_barrier_semaphore()
    pl.semaphore_signal(barrier, inc=1, device_id=partner, device_id_type=MESH)
    pl.semaphore_signal(barrier, inc=1, device_id=peer, device_id_type=MESH)

    @pl.when(has_fwd)
    def _():
        pl.semaphore_signal(barrier, inc=1, device_id=(fwd, s), device_id_type=MESH)

    @pl.when(has_bwd)
    def _():
        pl.semaphore_signal(barrier, inc=1, device_id=(bwd, s), device_id_type=MESH)

    def remote(kind, c, src, dst, device):
        return pltpu.make_async_remote_copy(
            src_ref=src,
            dst_ref=dst,
            send_sem=send_sem.at[kind, c],
            recv_sem=recv_sem.at[kind, c],
            device_id=device,
            device_id_type=MESH,
        )

    def both(c):
        return slice(c * LANES, (c + 1) * LANES)

    copy_a = [remote(0, c, s_a.at[c], r_a.at[c], partner) for c in range(2)]
    copy_h = [remote(1, c, s_h.at[c], r_h.at[c], (fwd, s)) for c in range(2)]
    copy_x0 = [remote(2, c, s_x.at[c, 0], r_x.at[c, 0], peer) for c in range(2)]
    copy_x1 = [remote(3, c, s_x.at[c, 1], r_x.at[c, 1], peer) for c in range(2)]
    copy_c = [remote(4, c, blur.at[c, core], blur.at[c, core], partner) for c in range(2)]
    copy_b = [remote(5, c, s_b.at[c], r_b.at[c], partner) for c in range(2)]
    copy_y = [remote(6, c, s_y.at[c], r_y.at[c], peer) for c in range(2)]
    copy_g = [
        remote(
            7, c, wide.at[c, core, :, pl.ds(far, 32)], wide.at[c, core, :, pl.ds(edge, 32)], (bwd, s)
        )
        for c in range(2)
    ]
    copy_d = [
        remote(
            8, c, wide.at[c, core, :, pl.ds(tile0, 64)], wide.at[c, core, :, pl.ds(tile0, 64)], partner
        )
        for c in range(2)
    ]
    copy_e = [
        remote(
            9, c, wide.at[c, core, :, pl.ds(edge, 32)], wide.at[c, core, :, pl.ds(edge, 32)], partner
        )
        for c in range(2)
    ]

    def partial(first, g):
        cells = lat[pl.ds(first + 4 * g, 4)].reshape(4 * SLAB, -1)
        narrow = mm(cells, kc[...]).astype(bf16)
        return mm(kri[core], narrow).reshape(4, WINDOW, 2 * LANES)

    bands = hy.shape[0]
    lead = lat.shape[0] * 16
    all_bands = basis_t.shape[1]
    spread_q = same((lat.shape[0], lead), plain, high).astype(bf16)
    spread_qt = same((lead, lat.shape[0]), high, plain).astype(bf16)
    tall = mm(spread_qt, basis_t[...]).astype(bf16)
    pick_t = same((all_bands, bands * 16), plain, lambda i: (i >> 4) + bands * s).astype(bf16)
    kbt[...] = (mm(tall, pick_t) * same((lead, bands * 16), low, low)).astype(bf16)

    loads[3].wait()

    def observed(at, width):
        return hy[:, at, width].reshape(bands * 16, -1)

    @pl.loop(0, SLAB // 16)
    def _(g):
        at = pl.ds(pl.multiple_of(16 * g, 16), 16)
        given = mm(kbt[pl.ds(16 * other, 16 * half)], observed(at, slice(None)))
        given = given.astype(bf16).reshape(half, 16, 2 * LANES)
        for c in range(2):
            s_b[c, :, at] = given[:, :, both(c)]

    pl.semaphore_wait(barrier, 2 + has_fwd.astype(jnp.int32) + has_bwd.astype(jnp.int32))
    for c in range(2):
        copy_b[c].start()

    loads[0].wait()

    @pl.loop(0, half // 4)
    def _(g):
        part = partial(other, g).astype(bf16)
        for c in range(2):
            s_a[c, pl.ds(4 * g, 4)] = part[:, :, both(c)]

    for c in range(2):
        copy_a[c].start()

    @pl.loop(0, SLAB // 16)
    def _(g):
        at = pl.ds(pl.multiple_of(16 * g, 16), 16)
        kept = mm(kbt[pl.ds(16 * mine, 16 * half)], observed(at, slice(None)))
        kept = kept.reshape(half, 16, 2 * LANES)
        for c in range(2):
            own_b[c, :, at] = kept[:, :, both(c)]

    def share(c):
        copy_b[c].wait_recv()
        total = own_b[c] + r_b[c].astype(f32)
        own_b[c] = total
        s_y[c] = total.astype(bf16)
        copy_y[c].start()

    share(0)
    loads[1].wait()

    @pl.loop(0, half // 4)
    def _(g):
        part = partial(mine, g)
        for c in range(2):
            own[c, pl.ds(4 * g, 4)] = part[:, :, both(c)]

    for c in range(2):
        copy_a[c].wait_recv()
        s_h[c] = (own[c, :, pl.ds(edge, 32)] + r_a[c, :, pl.ds(edge, 32)].astype(f32)).astype(bf16)

        @pl.when(has_fwd)
        def _():
            copy_h[c].start()

        mid = own[c, :, 32:64] + r_a[c, :, 32:64].astype(f32)
        own[c, :, 32:64] = mid
        s_x[c, 0] = mid.astype(bf16)
        copy_x0[c].start()
        own[c, :, pl.ds(far, 32)] = own[c, :, pl.ds(far, 32)] + r_a[c, :, pl.ds(far, 32)].astype(f32)

    repeated = jnp.broadcast_to(
        response[...].astype(f32)[:, None, :], (response.shape[0], 16, all_bands)
    )
    repeated = repeated.reshape(LANES, all_bands).astype(bf16)
    mixed = mm_nt(repeated, basis_t[...]).astype(bf16)
    km[...] = (mm(mixed, spread_q) * same((LANES, lead), low, low)).astype(bf16)
    kmt[...] = (mm_nt(tall, repeated) * same((lead, LANES), low, low)).astype(bf16)
    square = mm_nt(basis_t[...], basis_t[...])
    first = square.astype(bf16)
    second = (square - first.astype(f32)).astype(bf16)
    for k, part in enumerate((first, second)):
        grown = mm(mm(spread_qt, part).astype(bf16), spread_q)
        ks[k] = (grown * same((lead, lead), low, low)).astype(bf16)

    for c in range(2):

        @pl.when(has_bwd)
        def _():
            copy_h[c].wait_recv()
            own[c, :, pl.ds(far, 32)] = own[c, :, pl.ds(far, 32)] + r_h[c].astype(f32)

        s_x[c, 1] = own[c, :, pl.ds(far, 32)].astype(bf16)
        copy_x1[c].start()

    share(1)
    pick = same((bands * 16, all_bands), lambda i: (i >> 4) + bands * s, plain).astype(bf16)
    picked = mm_nt(pick, basis_t[...]).astype(bf16)
    kb[...] = (mm(picked, spread_q) * same((bands * 16, lead), low, low)).astype(bf16)
    loads[2].wait()

    @pl.loop(0, SLAB // 16)
    def _(g):
        at = pl.ds(pl.multiple_of(16 * g, 16), 16)
        for n in range(lat.shape[2] // 256):
            cut = slice(256 * n, 256 * n + 256)
            cells = lat[:, at, cut].reshape(lead, 256)
            resid = mm(km[...], cells) - mo[:, at, cut].reshape(LANES, 256).astype(f32)
            msr[:, at, cut] = resid.astype(bf16).reshape(-1, 16, 256)

    for c in range(2):
        copy_x0[c].wait_recv()
        blur[c, core, :, pl.ds(part1, 32)] = (
            own[c, :, pl.ds(far, 32)] + r_x[c, 0].astype(f32)
        ).astype(bf16)
        copy_x1[c].wait_recv()
        blur[c, core, :, pl.ds(part0, 32)] = (own[c, :, 32:64] + r_x[c, 1].astype(f32)).astype(bf16)
        copy_c[c].start()

    stores = [
        pltpu.make_async_copy(msr, ms_hbm, out_sem.at[0]),
        pltpu.make_async_copy(kmt, kmt_hbm, out_sem.at[1]),
    ]
    for store in stores:
        store.start()
    for c in range(2):
        copy_c[c].wait()
        copy_y[c].wait_recv()

        @pl.loop(0, SLAB // 16)
        def _(g):
            at = pl.ds(pl.multiple_of(16 * g, 16), 16)
            cells = blur[c, :, :, at].reshape(lead, LANES)
            rows = pl.ds(16 * mine, 16 * half)
            total = mm(ks[0, rows], cells) + mm(ks[1, rows], cells)
            total = total.reshape(half, 16, LANES) - own_b[c, :, at] - r_y[c, :, at].astype(f32)
            wide[c, core, :, pl.ds(pl.multiple_of(tile0 + 16 * g, 16), 16)] = total.astype(bf16)

        @pl.when(has_bwd)
        def _():
            copy_g[c].start()

        copy_d[c].start()

    @pl.loop(0, SLAB // 16)
    def _(g):
        at = pl.ds(pl.multiple_of(16 * g, 16), 16)
        cells = jnp.concatenate(
            [blur[c, :, :, at].reshape(lead, LANES) for c in range(2)], axis=1
        )
        resid = mm(kb[...], cells) - observed(at, slice(None)).astype(f32)
        hs[:, at] = resid.astype(bf16).reshape(bands, 16, 2 * LANES)

    stores.append(pltpu.make_async_copy(hs, hs_hbm, out_sem.at[2]))
    stores[2].start()

    for c in range(2):

        @pl.when(has_fwd)
        def _():
            copy_g[c].wait_recv()

        @pl.when(jnp.logical_not(has_fwd))
        def _():
            wide[c, core, :, pl.ds(edge, 32)] = jnp.zeros((half, 32, LANES), bf16)

        copy_e[c].start()

    def finish(first, who, slot):
        def group(g, carry):
            cells = jnp.concatenate(
                [wide[c, who, pl.ds(4 * g, 4)].reshape(4 * WINDOW, LANES) for c in range(2)], axis=1
            )
            rows = mm(krt[core], cells).astype(bf16)
            sp[pl.ds(first + 4 * g, 4)] = rows.reshape(4, SLAB, 2 * LANES)
            return carry

        lax.fori_loop(0, half // 4, group, 0)
        store = pltpu.make_async_copy(
            sp.at[pl.ds(first, half)], sp_hbm.at[pl.ds(first, half)], out_sem.at[slot]
        )
        store.start()
        stores.append(store)

    finish(mine, core, 3)
    for c in range(2):
        copy_d[c].wait_recv()
        copy_e[c].wait_recv()
    finish(other, 1 - core, 4)

    for c in range(2):
        for copies in (copy_a, copy_x0, copy_x1, copy_b, copy_y, copy_d, copy_e):
            copies[c].wait_send()

        @pl.when(has_fwd)
        def _():
            copy_h[c].wait_send()

        @pl.when(has_bwd)
        def _():
            copy_g[c].wait_send()

    for store in stores:
        store.wait()


def update(lat, sp, msr, kmt, kct, hs_from, z, hs_to, sem):
    passed = pltpu.make_async_copy(hs_from, hs_to, sem)

    @pl.when(pl.program_id(0) == 0)
    def _():
        passed.start()

    lead = lat.shape[0] * 16
    near = sp[...].reshape(lead, sp.shape[2])
    for n in range(lat.shape[2] // 256):
        cut = slice(256 * n, 256 * n + 256)
        back = mm(near, kct[:, cut]) + mm(kmt[...], msr[:, :, cut].reshape(LANES, 256))
        cells = lat[:, :, cut].reshape(lead, 256).astype(f32)
        z[:, :, cut] = (cells - STEP * back).astype(bf16).reshape(-1, 16, 256)

    @pl.when(pl.program_id(0) == pl.num_programs(0) - 1)
    def _():
        passed.wait()


def row_window(core):
    return kernel_values(
        SLAB * core + np.arange(SLAB)[None, :] - DECIM * np.arange(WINDOW)[:, None] + HALO
    )


def shards_joined(latent, basis, response, hyper_obs, multi_obs):
    cols = column_matrix(latent.shape[2])
    row = np.stack([np.kron(np.eye(4, dtype=np.float32), row_window(c).astype(np.float32)) for c in (0, 1)])
    row = row.astype(bf16)
    lead = latent.shape[0] * 16
    bands = hyper_obs.shape[0] * 16
    half = latent.shape[0] // 2
    coarse, low_cols = hyper_obs.shape[1:]

    def buf(shape, dtype=bf16):
        return pltpu.VMEM(shape, dtype)

    any_spec = pl.BlockSpec(memory_space=pl.ANY)
    vmem_spec = pl.BlockSpec(memory_space=pltpu.VMEM)
    spread, multi_resid, mix, residual = pl.pallas_call(
        joined,
        out_shape=(
            jax.ShapeDtypeStruct(latent.shape[:2] + (low_cols,), bf16),
            jax.ShapeDtypeStruct(multi_obs.shape, bf16),
            jax.ShapeDtypeStruct((lead, LANES), bf16),
            jax.ShapeDtypeStruct(hyper_obs.shape, bf16),
        ),
        in_specs=[any_spec] * 3 + [vmem_spec] * 5,
        out_specs=(any_spec,) * 4,
        scratch_shapes=[
            buf(latent.shape),
            buf(multi_obs.shape),
            buf(hyper_obs.shape),
            buf(latent.shape[:2] + (low_cols,)),
            buf(hyper_obs.shape),
            buf(multi_obs.shape),
            buf((bands, lead)),
            buf((lead, bands)),
            buf((LANES, lead)),
            buf((lead, LANES)),
            buf((2, lead, lead)),
            buf((2, half, WINDOW, LANES)),
            buf((2, half, WINDOW, LANES)),
            buf((2, half, WINDOW, LANES), f32),
            buf((2, half, 32, LANES)),
            buf((2, half, 32, LANES)),
            buf((2, 2, half, 32, LANES)),
            buf((2, 2, half, 32, LANES)),
            buf((2, 2, half, coarse, LANES)),
            buf((2, half, coarse, LANES)),
            buf((2, half, coarse, LANES)),
            buf((2, half, coarse, LANES), f32),
            buf((2, half, coarse, LANES)),
            buf((2, half, coarse, LANES)),
            buf((2, 2, half, WINDOW, LANES)),
            pltpu.SemaphoreType.DMA((4,)),
            pltpu.SemaphoreType.DMA((5,)),
            pltpu.SemaphoreType.DMA((10, 2)),
            pltpu.SemaphoreType.DMA((10, 2)),
        ],
        compiler_params=pltpu.CompilerParams(
            collective_id=0, has_side_effects=True, vmem_limit_bytes=56 * 1024 * 1024
        ),
        cost_estimate=pl.CostEstimate(
            flops=10 * 1024**3, bytes_accessed=13 * 1024 * 1024, transcendentals=0
        ),
        name="joined",
    )(
        latent,
        multi_obs,
        hyper_obs,
        basis.T,
        response,
        jnp.asarray(cols),
        jnp.asarray(row),
        jnp.asarray(row.transpose(0, 2, 1)),
    )
    rows = 16
    full = latent.shape[2]
    return pl.pallas_call(
        update,
        grid=(latent.shape[1] // rows,),
        out_shape=(
            jax.ShapeDtypeStruct(latent.shape, bf16),
            jax.ShapeDtypeStruct(hyper_obs.shape, bf16),
        ),
        in_specs=[
            pl.BlockSpec((latent.shape[0], rows, full), lambda g: (0, g, 0)),
            pl.BlockSpec((latent.shape[0], rows, low_cols), lambda g: (0, g, 0)),
            pl.BlockSpec((multi_obs.shape[0], rows, full), lambda g: (0, g, 0)),
            pl.BlockSpec((lead, LANES), lambda g: (0, 0)),
            pl.BlockSpec((low_cols, full), lambda g: (0, 0)),
            any_spec,
        ],
        out_specs=(
            pl.BlockSpec((latent.shape[0], rows, full), lambda g: (0, g, 0)),
            any_spec,
        ),
        scratch_shapes=[pltpu.SemaphoreType.DMA(())],
        compiler_params=pltpu.CompilerParams(vmem_limit_bytes=32 * 1024 * 1024),
        name="update",
    )(latent, spread, multi_resid, mix, jnp.asarray(cols.T), residual)


def shards(latent, basis, response, hyper_obs, multi_obs):
    fits = (
        lax.axis_size("spec") == N_SPEC
        and latent.shape == (32, SLAB, 1024)
        and hyper_obs.shape[1:] == (SLAB, 2 * LANES)
    )
    run = shards_joined if fits else shards_plain
    return run(latent, basis, response, hyper_obs, multi_obs)


def solution(mesh):
    in_specs = (
        P(None, ("tile", "spec"), None),
        P(),
        P(),
        P("spec", "tile", None),
        P(None, ("tile", "spec"), None),
    )
    out_specs = (P(None, ("tile", "spec"), None), P("spec", "tile", None))
    return jax.shard_map(shards, mesh=mesh, in_specs=in_specs, out_specs=out_specs, check_vma=False)
```

```python
import jax
import jax.numpy as jnp
import numpy as np
from jax import lax
from jax.experimental import pallas as pl
from jax.experimental.pallas import tpu as pltpu
from jax.sharding import PartitionSpec as P

DECIM = 4
HALO = 128
RIM = HALO // DECIM
STEP = 0.3


def profile(where_at):
    narrow = np.float32(DECIM / 2.0)
    decay_len = np.float32(3.0 * HALO / 8.0)
    ripple = np.cos(where_at * np.float32(np.pi / 7.0))
    return np.exp(-where_at * where_at / (np.float32(2.0) * narrow * narrow)) + np.float32(
        0.5
    ) * np.exp(-np.abs(where_at) / decay_len) * ripple * ripple


def kernel_values(offsets):
    every_offset = np.arange(-HALO, HALO + 1).astype(np.float32)
    energy = np.sqrt(np.sum(profile(every_offset) ** 2))
    inside = np.abs(offsets) <= HALO
    return np.where(inside, profile(offsets.astype(np.float32)) / energy, np.float32(0.0)).astype(
        jnp.bfloat16
    )


def column_matrix(fine_count):
    return kernel_values(np.arange(fine_count)[:, None] - DECIM * np.arange(fine_count // DECIM)[None, :])


def dot(spec, a, b):
    return jnp.einsum(spec, a, b, preferred_element_type=jnp.float32)


def shards_plain(latent, basis, response, hyper_obs, multi_obs):
    bf16 = jnp.bfloat16
    f32 = jnp.float32
    group = hyper_obs.shape[0]
    coarse = hyper_obs.shape[1]
    rows_dev = coarse * DECIM
    count = lax.axis_size("tile")
    up = [(i + 1, i) for i in range(count - 1)]
    down = [(i, i + 1) for i in range(count - 1)]
    cols = column_matrix(latent.shape[2])
    rows = kernel_values(
        np.arange(rows_dev)[:, None] - DECIM * (np.arange(coarse + 2 * RIM)[None, :] - RIM)
    )
    cols = jnp.asarray(cols)
    rows = jnp.asarray(rows)

    narrow = dot("qrc,cj->qrj", latent, cols).astype(bf16)
    narrow = lax.all_to_all(narrow, "spec", split_axis=0, concat_axis=1, tiled=True)
    part = dot("ri,qrj->qij", rows, narrow)
    above = lax.ppermute(part[:, :RIM].astype(bf16), "tile", up)
    below = lax.ppermute(part[:, RIM + coarse :].astype(bf16), "tile", down)
    own = part[:, RIM : RIM + coarse]
    zeros = jnp.zeros((own.shape[0], coarse - RIM, own.shape[2]), f32)
    own = (
        own
        + jnp.concatenate([below.astype(f32), zeros], axis=1)
        + jnp.concatenate([zeros, above.astype(f32)], axis=1)
    ).astype(bf16)
    blurred = lax.all_gather(own, "spec", axis=0, tiled=True)
    mine = lax.dynamic_slice_in_dim(basis, lax.axis_index("spec") * group, group, 0)
    hs_residual = (dot("bq,qij->bij", mine, blurred) - hyper_obs.astype(f32)).astype(bf16)
    back = dot("bq,bij->qij", mine, hs_residual).astype(bf16)
    back = lax.all_to_all(back, "spec", split_axis=0, concat_axis=0, tiled=True)
    back = back.reshape((lax.axis_size("spec"), -1) + back.shape[1:])
    back = jnp.sum(back.astype(f32), axis=0).astype(bf16)
    from_below = lax.ppermute(back[:, :RIM], "tile", up)
    from_above = lax.ppermute(back[:, coarse - RIM :], "tile", down)
    padded = jnp.concatenate([from_above, back, from_below], axis=1)
    rows_back = dot("ri,qij->qrj", rows, padded).astype(bf16)
    rows_back = lax.all_to_all(rows_back, "spec", split_axis=1, concat_axis=0, tiled=True)
    spread = dot("qrj,cj->qrc", rows_back, cols)
    mixed = dot("mb,bq->mq", response, basis).astype(bf16)
    multi_resid = (dot("mq,qrc->mrc", mixed, latent) - multi_obs.astype(f32)).astype(bf16)
    gradient = spread + dot("mq,mrc->qrc", mixed, multi_resid)
    z_next = (latent.astype(f32) - STEP * gradient).astype(bf16)
    return (z_next, hs_residual)


N_SPEC = 4
SLAB = 64
WINDOW = 96
LANES = 128
MESH = pl.DeviceIdType.MESH
bf16 = jnp.bfloat16
f32 = jnp.float32


def mm(a, b):
    return jnp.dot(a, b, preferred_element_type=f32)


def mm_nt(a, b):
    return lax.dot_general(a, b, (((1,), (1,)), ((), ())), preferred_element_type=f32)


def same(shape, row_of, col_of):
    rows = row_of(lax.broadcasted_iota(jnp.int32, shape, 0))
    cols = col_of(lax.broadcasted_iota(jnp.int32, shape, 1))
    return jnp.where(rows == cols, 1.0, 0.0)


def low(i):
    return i & 15


def high(i):
    return i >> 4


def plain(i):
    return i


def joined(
    lat_hbm, mo_hbm, hy_hbm, basis_t, response, kc, kri, krt,
    sp_hbm, ms_hbm, kmt_hbm, hs_hbm,
    lat, mo, hy, sp, hs, msr, kb, kbt, km, kmt, ks,
    s_a, r_a, own, s_h, r_h, s_x, r_x, blur, s_b, r_b, own_b, s_y, r_y, wide,
    in_sem, out_sem, send_sem, recv_sem,
):
    t = lax.axis_index("tile")
    s = lax.axis_index("spec")
    count = lax.axis_size("tile")
    x, core = s // 2, s % 2
    half = lat.shape[0] // 2
    partner = (t, 2 * x + 1 - core)
    peer = (t, 2 * (1 - x) + core)
    fwd, bwd = t - 1 + 2 * x, t + 1 - 2 * x
    has_fwd = jnp.logical_and(fwd >= 0, fwd < count)
    has_bwd = jnp.logical_and(bwd >= 0, bwd < count)
    mine = pl.multiple_of(half * core, half)
    other = pl.multiple_of(half * (1 - core), half)
    edge = pl.multiple_of(64 * x, 32)
    far = pl.multiple_of(64 * (1 - x), 32)
    tile0 = pl.multiple_of(32 * (1 - x), 32)
    part0 = pl.multiple_of(32 * x, 32)
    part1 = pl.multiple_of(32 * (1 - x), 32)

    loads = [
        pltpu.make_async_copy(
            lat_hbm.at[pl.ds(other, half)], lat.at[pl.ds(other, half)], in_sem.at[0]
        ),
        pltpu.make_async_copy(
            lat_hbm.at[pl.ds(mine, half)], lat.at[pl.ds(mine, half)], in_sem.at[1]
        ),
        pltpu.make_async_copy(mo_hbm, mo, in_sem.at[2]),
        pltpu.make_async_copy(hy_hbm, hy, in_sem.at[3]),
    ]
    for load in (loads[3], loads[0], loads[1], loads[2]):
        load.start()

    barrier = pltpu.get_barrier_semaphore()
    pl.semaphore_signal(barrier, inc=1, device_id=partner, device_id_type=MESH)
    pl.semaphore_signal(barrier, inc=1, device_id=peer, device_id_type=MESH)

    @pl.when(has_fwd)
    def _():
        pl.semaphore_signal(barrier, inc=1, device_id=(fwd, s), device_id_type=MESH)

    @pl.when(has_bwd)
    def _():
        pl.semaphore_signal(barrier, inc=1, device_id=(bwd, s), device_id_type=MESH)

    def remote(kind, c, src, dst, device):
        return pltpu.make_async_remote_copy(
            src_ref=src,
            dst_ref=dst,
            send_sem=send_sem.at[kind, c],
            recv_sem=recv_sem.at[kind, c],
            device_id=device,
            device_id_type=MESH,
        )

    def both(c):
        return slice(c * LANES, (c + 1) * LANES)

    copy_a = [remote(0, c, s_a.at[c], r_a.at[c], partner) for c in range(2)]
    copy_h = [remote(1, c, s_h.at[c], r_h.at[c], (fwd, s)) for c in range(2)]
    copy_x0 = [remote(2, c, s_x.at[c, 0], r_x.at[c, 0], peer) for c in range(2)]
    copy_x1 = [remote(3, c, s_x.at[c, 1], r_x.at[c, 1], peer) for c in range(2)]
    copy_c = [remote(4, c, blur.at[c, core], blur.at[c, core], partner) for c in range(2)]
    copy_b = [remote(5, c, s_b.at[c], r_b.at[c], partner) for c in range(2)]
    copy_y = [remote(6, c, s_y.at[c], r_y.at[c], peer) for c in range(2)]
    copy_g = [
        remote(
            7, c, wide.at[c, core, :, pl.ds(far, 32)], wide.at[c, core, :, pl.ds(edge, 32)], (bwd, s)
        )
        for c in range(2)
    ]
    copy_d = [
        remote(
            8, c, wide.at[c, core, :, pl.ds(tile0, 64)], wide.at[c, core, :, pl.ds(tile0, 64)], partner
        )
        for c in range(2)
    ]
    copy_e = [
        remote(
            9, c, wide.at[c, core, :, pl.ds(edge, 32)], wide.at[c, core, :, pl.ds(edge, 32)], partner
        )
        for c in range(2)
    ]

    def partial(first, g):
        cells = lat[pl.ds(first + 4 * g, 4)].reshape(4 * SLAB, -1)
        narrow = mm(cells, kc[...]).astype(bf16)
        return mm(kri[core], narrow).reshape(4, WINDOW, 2 * LANES)

    bands = hy.shape[0]
    lead = lat.shape[0] * 16
    all_bands = basis_t.shape[1]
    spread_q = same((lat.shape[0], lead), plain, high).astype(bf16)
    spread_qt = same((lead, lat.shape[0]), high, plain).astype(bf16)
    tall = mm(spread_qt, basis_t[...]).astype(bf16)
    pick_t = same((all_bands, bands * 16), plain, lambda i: (i >> 4) + bands * s).astype(bf16)
    kbt[...] = (mm(tall, pick_t) * same((lead, bands * 16), low, low)).astype(bf16)

    loads[3].wait()

    def observed(at, width):
        return hy[:, at, width].reshape(bands * 16, -1)

    @pl.loop(0, SLAB // 16)
    def _(g):
        at = pl.ds(pl.multiple_of(16 * g, 16), 16)
        given = mm(kbt[pl.ds(16 * other, 16 * half)], observed(at, slice(None)))
        given = given.astype(bf16).reshape(half, 16, 2 * LANES)
        for c in range(2):
            s_b[c, :, at] = given[:, :, both(c)]

    pl.semaphore_wait(barrier, 2 + has_fwd.astype(jnp.int32) + has_bwd.astype(jnp.int32))
    for c in range(2):
        copy_b[c].start()

    loads[0].wait()

    @pl.loop(0, half // 4)
    def _(g):
        part = partial(other, g).astype(bf16)
        for c in range(2):
            s_a[c, pl.ds(4 * g, 4)] = part[:, :, both(c)]

    for c in range(2):
        copy_a[c].start()

    @pl.loop(0, SLAB // 16)
    def _(g):
        at = pl.ds(pl.multiple_of(16 * g, 16), 16)
        kept = mm(kbt[pl.ds(16 * mine, 16 * half)], observed(at, slice(None)))
        kept = kept.reshape(half, 16, 2 * LANES)
        for c in range(2):
            own_b[c, :, at] = kept[:, :, both(c)]

    def share(c):
        copy_b[c].wait_recv()
        total = own_b[c] + r_b[c].astype(f32)
        own_b[c] = total
        s_y[c] = total.astype(bf16)
        copy_y[c].start()

    share(0)
    loads[1].wait()

    @pl.loop(0, half // 4)
    def _(g):
        part = partial(mine, g)
        for c in range(2):
            own[c, pl.ds(4 * g, 4)] = part[:, :, both(c)]

    for c in range(2):
        copy_a[c].wait_recv()
        s_h[c] = (own[c, :, pl.ds(edge, 32)] + r_a[c, :, pl.ds(edge, 32)].astype(f32)).astype(bf16)

        @pl.when(has_fwd)
        def _():
            copy_h[c].start()

        mid = own[c, :, 32:64] + r_a[c, :, 32:64].astype(f32)
        own[c, :, 32:64] = mid
        s_x[c, 0] = mid.astype(bf16)
        copy_x0[c].start()
        own[c, :, pl.ds(far, 32)] = own[c, :, pl.ds(far, 32)] + r_a[c, :, pl.ds(far, 32)].astype(f32)

    repeated = jnp.broadcast_to(
        response[...].astype(f32)[:, None, :], (response.shape[0], 16, all_bands)
    )
    repeated = repeated.reshape(LANES, all_bands).astype(bf16)
    mixed = mm_nt(repeated, basis_t[...]).astype(bf16)
    km[...] = (mm(mixed, spread_q) * same((LANES, lead), low, low)).astype(bf16)
    kmt[...] = (mm_nt(tall, repeated) * same((lead, LANES), low, low)).astype(bf16)
    square = mm_nt(basis_t[...], basis_t[...])
    first = square.astype(bf16)
    second = (square - first.astype(f32)).astype(bf16)
    for k, part in enumerate((first, second)):
        grown = mm(mm(spread_qt, part).astype(bf16), spread_q)
        ks[k] = (grown * same((lead, lead), low, low)).astype(bf16)

    for c in range(2):

        @pl.when(has_bwd)
        def _():
            copy_h[c].wait_recv()
            own[c, :, pl.ds(far, 32)] = own[c, :, pl.ds(far, 32)] + r_h[c].astype(f32)

        s_x[c, 1] = own[c, :, pl.ds(far, 32)].astype(bf16)
        copy_x1[c].start()

    share(1)
    pick = same((bands * 16, all_bands), lambda i: (i >> 4) + bands * s, plain).astype(bf16)
    picked = mm_nt(pick, basis_t[...]).astype(bf16)
    kb[...] = (mm(picked, spread_q) * same((bands * 16, lead), low, low)).astype(bf16)
    loads[2].wait()

    @pl.loop(0, SLAB // 16)
    def _(g):
        at = pl.ds(pl.multiple_of(16 * g, 16), 16)
        for n in range(lat.shape[2] // 256):
            cut = slice(256 * n, 256 * n + 256)
            cells = lat[:, at, cut].reshape(lead, 256)
            resid = mm(km[...], cells) - mo[:, at, cut].reshape(LANES, 256).astype(f32)
            msr[:, at, cut] = resid.astype(bf16).reshape(-1, 16, 256)

    for c in range(2):
        copy_x0[c].wait_recv()
        blur[c, core, :, pl.ds(part1, 32)] = (
            own[c, :, pl.ds(far, 32)] + r_x[c, 0].astype(f32)
        ).astype(bf16)
        copy_x1[c].wait_recv()
        blur[c, core, :, pl.ds(part0, 32)] = (own[c, :, 32:64] + r_x[c, 1].astype(f32)).astype(bf16)
        copy_c[c].start()

    stores = [
        pltpu.make_async_copy(msr, ms_hbm, out_sem.at[0]),
        pltpu.make_async_copy(kmt, kmt_hbm, out_sem.at[1]),
    ]
    for store in stores:
        store.start()
    for c in range(2):
        copy_c[c].wait()
        copy_y[c].wait_recv()

        @pl.loop(0, SLAB // 16)
        def _(g):
            at = pl.ds(pl.multiple_of(16 * g, 16), 16)
            cells = blur[c, :, :, at].reshape(lead, LANES)
            rows = pl.ds(16 * mine, 16 * half)
            total = mm(ks[0, rows], cells) + mm(ks[1, rows], cells)
            total = total.reshape(half, 16, LANES) - own_b[c, :, at] - r_y[c, :, at].astype(f32)
            wide[c, core, :, pl.ds(pl.multiple_of(tile0 + 16 * g, 16), 16)] = total.astype(bf16)

        @pl.when(has_bwd)
        def _():
            copy_g[c].start()

        copy_d[c].start()

    @pl.loop(0, SLAB // 16)
    def _(g):
        at = pl.ds(pl.multiple_of(16 * g, 16), 16)
        cells = jnp.concatenate(
            [blur[c, :, :, at].reshape(lead, LANES) for c in range(2)], axis=1
        )
        resid = mm(kb[...], cells) - observed(at, slice(None)).astype(f32)
        hs[:, at] = resid.astype(bf16).reshape(bands, 16, 2 * LANES)

    stores.append(pltpu.make_async_copy(hs, hs_hbm, out_sem.at[2]))
    stores[2].start()

    for c in range(2):

        @pl.when(has_fwd)
        def _():
            copy_g[c].wait_recv()

        @pl.when(jnp.logical_not(has_fwd))
        def _():
            wide[c, core, :, pl.ds(edge, 32)] = jnp.zeros((half, 32, LANES), bf16)

        copy_e[c].start()

    def finish(first, who, slot):
        def group(g, carry):
            cells = jnp.concatenate(
                [wide[c, who, pl.ds(4 * g, 4)].reshape(4 * WINDOW, LANES) for c in range(2)], axis=1
            )
            rows = mm(krt[core], cells).astype(bf16)
            sp[pl.ds(first + 4 * g, 4)] = rows.reshape(4, SLAB, 2 * LANES)
            return carry

        lax.fori_loop(0, half // 4, group, 0)
        store = pltpu.make_async_copy(
            sp.at[pl.ds(first, half)], sp_hbm.at[pl.ds(first, half)], out_sem.at[slot]
        )
        store.start()
        stores.append(store)

    finish(mine, core, 3)
    for c in range(2):
        copy_d[c].wait_recv()
        copy_e[c].wait_recv()
    finish(other, 1 - core, 4)

    for c in range(2):
        for copies in (copy_a, copy_x0, copy_x1, copy_b, copy_y, copy_d, copy_e):
            copies[c].wait_send()

        @pl.when(has_fwd)
        def _():
            copy_h[c].wait_send()

        @pl.when(has_bwd)
        def _():
            copy_g[c].wait_send()

    for store in stores:
        store.wait()


def update(lat, sp, msr, kmt, kct, hs_from, z, hs_to, sem):
    passed = pltpu.make_async_copy(hs_from, hs_to, sem)

    @pl.when(pl.program_id(0) == 0)
    def _():
        passed.start()

    lead = lat.shape[0] * 16
    near = sp[...].reshape(lead, sp.shape[2])
    for n in range(lat.shape[2] // 256):
        cut = slice(256 * n, 256 * n + 256)
        back = mm(near, kct[:, cut]) + mm(kmt[...], msr[:, :, cut].reshape(LANES, 256))
        cells = lat[:, :, cut].reshape(lead, 256).astype(f32)
        z[:, :, cut] = (cells - STEP * back).astype(bf16).reshape(-1, 16, 256)

    @pl.when(pl.program_id(0) == pl.num_programs(0) - 1)
    def _():
        passed.wait()


def row_window(core):
    return kernel_values(
        SLAB * core + np.arange(SLAB)[None, :] - DECIM * np.arange(WINDOW)[:, None] + HALO
    )


def shards_joined(latent, basis, response, hyper_obs, multi_obs):
    cols = column_matrix(latent.shape[2])
    row = np.stack([np.kron(np.eye(4, dtype=np.float32), row_window(c).astype(np.float32)) for c in (0, 1)])
    row = row.astype(bf16)
    lead = latent.shape[0] * 16
    bands = hyper_obs.shape[0] * 16
    half = latent.shape[0] // 2
    coarse, low_cols = hyper_obs.shape[1:]

    def buf(shape, dtype=bf16):
        return pltpu.VMEM(shape, dtype)

    any_spec = pl.BlockSpec(memory_space=pl.ANY)
    vmem_spec = pl.BlockSpec(memory_space=pltpu.VMEM)
    spread, multi_resid, mix, residual = pl.pallas_call(
        joined,
        out_shape=(
            jax.ShapeDtypeStruct(latent.shape[:2] + (low_cols,), bf16),
            jax.ShapeDtypeStruct(multi_obs.shape, bf16),
            jax.ShapeDtypeStruct((lead, LANES), bf16),
            jax.ShapeDtypeStruct(hyper_obs.shape, bf16),
        ),
        in_specs=[any_spec] * 3 + [vmem_spec] * 5,
        out_specs=(any_spec,) * 4,
        scratch_shapes=[
            buf(latent.shape),
            buf(multi_obs.shape),
            buf(hyper_obs.shape),
            buf(latent.shape[:2] + (low_cols,)),
            buf(hyper_obs.shape),
            buf(multi_obs.shape),
            buf((bands, lead)),
            buf((lead, bands)),
            buf((LANES, lead)),
            buf((lead, LANES)),
            buf((2, lead, lead)),
            buf((2, half, WINDOW, LANES)),
            buf((2, half, WINDOW, LANES)),
            buf((2, half, WINDOW, LANES), f32),
            buf((2, half, 32, LANES)),
            buf((2, half, 32, LANES)),
            buf((2, 2, half, 32, LANES)),
            buf((2, 2, half, 32, LANES)),
            buf((2, 2, half, coarse, LANES)),
            buf((2, half, coarse, LANES)),
            buf((2, half, coarse, LANES)),
            buf((2, half, coarse, LANES), f32),
            buf((2, half, coarse, LANES)),
            buf((2, half, coarse, LANES)),
            buf((2, 2, half, WINDOW, LANES)),
            pltpu.SemaphoreType.DMA((4,)),
            pltpu.SemaphoreType.DMA((5,)),
            pltpu.SemaphoreType.DMA((10, 2)),
            pltpu.SemaphoreType.DMA((10, 2)),
        ],
        compiler_params=pltpu.CompilerParams(
            collective_id=0, has_side_effects=True, vmem_limit_bytes=56 * 1024 * 1024
        ),
        cost_estimate=pl.CostEstimate(
            flops=10 * 1024**3, bytes_accessed=13 * 1024 * 1024, transcendentals=0
        ),
        name="joined",
    )(
        latent,
        multi_obs,
        hyper_obs,
        basis.T,
        response,
        jnp.asarray(cols),
        jnp.asarray(row),
        jnp.asarray(row.transpose(0, 2, 1)),
    )
    rows = 16
    full = latent.shape[2]
    return pl.pallas_call(
        update,
        grid=(latent.shape[1] // rows,),
        out_shape=(
            jax.ShapeDtypeStruct(latent.shape, bf16),
            jax.ShapeDtypeStruct(hyper_obs.shape, bf16),
        ),
        in_specs=[
            pl.BlockSpec((latent.shape[0], rows, full), lambda g: (0, g, 0)),
            pl.BlockSpec((latent.shape[0], rows, low_cols), lambda g: (0, g, 0)),
            pl.BlockSpec((multi_obs.shape[0], rows, full), lambda g: (0, g, 0)),
            pl.BlockSpec((lead, LANES), lambda g: (0, 0)),
            pl.BlockSpec((low_cols, full), lambda g: (0, 0)),
            any_spec,
        ],
        out_specs=(
            pl.BlockSpec((latent.shape[0], rows, full), lambda g: (0, g, 0)),
            any_spec,
        ),
        scratch_shapes=[pltpu.SemaphoreType.DMA(())],
        compiler_params=pltpu.CompilerParams(vmem_limit_bytes=62 * 1024 * 1024),
        name="update",
    )(latent, spread, multi_resid, mix, jnp.asarray(cols.T), residual)


def shards(latent, basis, response, hyper_obs, multi_obs):
    fits = (
        lax.axis_size("spec") == N_SPEC
        and latent.shape == (32, SLAB, 1024)
        and hyper_obs.shape[1:] == (SLAB, 2 * LANES)
    )
    run = shards_joined if fits else shards_plain
    return run(latent, basis, response, hyper_obs, multi_obs)


def solution(mesh):
    in_specs = (
        P(None, ("tile", "spec"), None),
        P(),
        P(),
        P("spec", "tile", None),
        P(None, ("tile", "spec"), None),
    )
    out_specs = (P(None, ("tile", "spec"), None), P("spec", "tile", None))
    return jax.shard_map(shards, mesh=mesh, in_specs=in_specs, out_specs=out_specs, check_vma=False)
```
